128 devices in a mesh: shard: 32 (over x, y, core), rep: 4 (over z).
Axes of the slice: x: 4, y: 4, z: 4, core: 2. Of those that a mesh axis runs over, the one named last changes fastest.
Arguments:
- queries: bfloat16 [24576, 256], P(('shard', 'rep')), may hold values from -6 to 6
- item_owner: int32 [24576, 1], P(('shard', 'rep')), may hold values from 0 to 31; in each aligned block of 192 rows (0 to 191, 192 to 383, ...) at most 12 rows name the same one
- item_row: int32 [24576], P(('shard', 'rep')), may hold values from 0 to 2047
- log_freq: bfloat16 [24576], P(('shard', 'rep')), may hold values from -9 to -3
- table: float32 [65536, 256], P('shard'), may hold values from -6 to 6
- accum: float32 [65536, 256], P('shard'), may hold values from 0.001 to 0.1
- w_in: bfloat16 [256, 512], replicated, may hold values from -0.375 to 0.375
- w_out: bfloat16 [512, 256], replicated, may hold values from -0.25 to 0.25
Outputs:
- query_grad: float32 [24576, 256], P(('shard', 'rep'))
- table_new: float32 [65536, 256], P('shard')
- accum_new: float32 [65536, 256], P('shard')
- w_in_grad: float32 [256, 512], replicated
- w_out_grad: float32 [512, 256], replicated
The draws below stay inside these ranges and needn't reach their ends.
Inputs may be any that keep to these rules, and one draw needn't show every extreme that they name: `item_owner`: among the pairs of one device no owner is named more than 12 times, a bound that some block reaches.
All inputs are finite; a program needn't handle non-finite values.
Results may differ from the reference program's by a relative error of at most 0.0039.
The reference program's roundings to bfloat16 on the way (of `emb`, `hidden`, `vec`, `coef`, `vec_grad` and `hidden_grad`) count: a program that leaves them out, or rounds other values in their place, can miss the bound.
Values may be sent and summed in bfloat16 or wider, within the bound.
No kernel may reach another device: no remote copies, remote signals or barrier semaphores. Data moves between devices by JAX's collectives and lax.ppermute only.
A program may use at most 128 MiB of HBM per device.

```python
import math
import jax
import jax.numpy as jnp
import numpy as np
from jax import lax

E = 256
H = 512
PAIRS_DEV = 192
ROWS_DEV = 2048
CAP = 12
PAIRS = 24576
ROWS = 65536
N_SHARD = 32


def plant(result, own_key, low, top_value):
    place = [jax.random.randint(jax.random.fold_in(own_key, axis), (), 0, length) for axis, length in enumerate(result.shape)]
    main_axis = result.shape.index(max(result.shape))
    neighbour = place[:main_axis] + [(place[main_axis] + 1) % result.shape[main_axis]] + place[main_axis + 1:]
    return result.at[tuple(place)].set(low).at[tuple(neighbour)].set(top_value)


def block_levels(key, extent, split, least, high):
    loudness, own = 1.0, jax.random.fold_in(key, 6)
    for position, shards_of in split:
        heights = jnp.exp(jax.random.uniform(jax.random.fold_in(own, position), (shards_of,), jnp.float32, least / len(split), high / len(split)))
        loudness = loudness * jnp.repeat(heights, extent[position] // shards_of).reshape([-1 if axis == position else 1 for axis in range(len(extent))])
    return loudness


def routed_block(rng, own, number, rows, count, top, reach, slope):
    order = jax.random.permutation(rng, count)
    packed, ordinary = load_shares(count, rows * top, reach, slope, True), load_shares(count, rows * top, reach, slope, False)
    places = jnp.arange(count)

    def named(lengths, turn):
        used = int((lengths > 0).sum())
        fixed = max(1, used // 4)
        moved = fixed + (places - fixed + turn * (used - fixed)) % max(1, count - fixed)
        return jnp.zeros((count,), jnp.int32).at[order[jnp.where(places < fixed, places, moved)]].set(jnp.asarray(lengths, jnp.int32))

    lengths = jnp.where(number % 4 == 0, named(packed, number // 4), named(ordinary, number - number // 4 - 1))
    mixed = jax.random.permutation(jax.random.fold_in(own, 3), count)
    source_of, sink = mixed[0:count // 2 * 2:2], mixed[1:count // 2 * 2:2]
    margin = jnp.minimum(lengths[source_of] - 1, reach - lengths[sink]) // 2
    margin = jnp.where((source_of == order[0]) | (sink == order[0]) | (lengths[sink] == 0), 0, jnp.maximum(margin, 0))
    moved = jax.random.randint(jax.random.fold_in(own, 4), (count // 2,), 0, 1 << 20) % (margin + 1)
    lengths = lengths.at[source_of].add(-moved).at[sink].add(moved)
    items = jnp.searchsorted(jnp.cumsum(lengths), jnp.arange(rows * top), side="right").astype(jnp.int32)
    grid = items.reshape(top, rows).T
    grid = grid[jax.random.permutation(jax.random.fold_in(own, 1), rows)]
    turn = jax.random.randint(jax.random.fold_in(own, 2), (rows, 1), 0, top)
    return jnp.take_along_axis(grid, (jnp.arange(top)[None, :] + turn) % top, axis=1)


def load_shares(amount, total, limit, lean, full):
    weights = [(1 << 20) // math.isqrt(rank ** lean) + 1 for rank in range(1, amount + 1)]
    largest = limit if full else min(limit, max(-(-total // amount), total * weights[0] // sum(weights)))
    least = 1 if total - largest >= amount - 1 else 0
    counts, rest = [largest] + [least] * (amount - 1), total - largest - least * (amount - 1)
    while rest > 0:
        movable = [i for i in range(1, amount) if counts[i] < largest] or [i for i in range(1, amount) if counts[i] < limit]
        mass, remaining = sum([weights[i] for i in movable]), rest
        for i in movable:
            more = min(limit - counts[i], max(1, remaining * weights[i] // mass), rest)
            counts[i] = counts[i] + more
            rest = rest - more
    return np.array(counts)


def normal_values(key, extent, width, reach, shards=(), held_as=jnp.bfloat16):
    loudness = block_levels(key, extent, shards, -0.22, 0.18) if shards else 1.0
    drawn = jax.random.normal(key, extent, jnp.float32) * width * loudness
    return jnp.minimum(jnp.maximum(drawn, -reach), reach).astype(held_as)


def setup_inputs(seed: int = 0) -> dict:
    keys = jax.random.split(jax.random.key(seed), 9)
    queries = normal_values(keys[0], (PAIRS, E), 1.0, 6.0, ((0, 128),))
    item_owner_keys = jax.random.split(jax.random.fold_in(keys[1], 1), PAIRS // PAIRS_DEV)
    item_owner_turns = jax.random.permutation(jax.random.fold_in(keys[1], 3), PAIRS // PAIRS_DEV)
    item_owner = jax.vmap(lambda own, number: routed_block(jax.random.fold_in(keys[1], 2), own, number, PAIRS_DEV, N_SHARD, 1, CAP, 2))(item_owner_keys, item_owner_turns).reshape((PAIRS, 1))
    item_row = plant(jax.random.randint(keys[2], (PAIRS,), 0, ROWS_DEV), jax.random.fold_in(keys[2], 1), 0, ROWS_DEV - 1).astype(jnp.int32)
    log_freq = jnp.clip(-9.0 + 6.0 * jax.random.uniform(keys[3], (PAIRS,), jnp.float32) ** block_levels(keys[3], (PAIRS,), ((0, 128),), -0.2, 0.2), -9.0, -3.0).astype(jnp.bfloat16)
    table = normal_values(keys[4], (ROWS, E), 1.0, 6.0, ((0, 32),), jnp.float32)
    accum = jnp.clip(jnp.exp(math.log(0.1) - 4.6051702 * jax.random.uniform(keys[5], (ROWS, E), jnp.float32) ** block_levels(keys[5], (ROWS, E), ((0, 32),), -0.2, 0.2)), 0.001, 0.1)
    w_in = normal_values(keys[6], (E, H), E ** -0.5, 0.375)
    w_out = normal_values(keys[7], (H, E), H ** -0.5, 0.25)
    return {"queries": queries, "item_owner": item_owner, "item_row": item_row, "log_freq": log_freq, "table": table, "accum": accum, "w_in": w_in, "w_out": w_out}


score_scale = 0.0625
learn_rate = 0.1

def reference(queries, item_owner, item_row, log_freq, table, accum, w_in, w_out):
    item_id = item_owner[:, 0] * ROWS_DEV + item_row
    emb = table[item_id].astype(jnp.bfloat16)
    hidden = jax.nn.relu(jnp.dot(emb, w_in, preferred_element_type=jnp.float32)).astype(jnp.bfloat16)
    vec = (emb.astype(jnp.float32) + jnp.dot(hidden, w_out, preferred_element_type=jnp.float32)).astype(jnp.bfloat16)
    freq = log_freq.astype(jnp.float32)
    block = min(1024, PAIRS)
    count = PAIRS // block

    def step(carry, index):
        start = (index * block).astype(jnp.int32)
        query_block = lax.dynamic_slice_in_dim(queries, start, block, 0)
        scores = jnp.dot(query_block, vec.T, preferred_element_type=jnp.float32) * score_scale - freq[None, :]
        top = lax.optimization_barrier(jnp.max(scores, axis=1))
        lse = top + jnp.log(lax.optimization_barrier(jnp.sum(jnp.exp(scores - top[:, None]), axis=1)))
        rows = start + jnp.arange(block, dtype=jnp.int32)
        diagonal = (rows[:, None] == jnp.arange(PAIRS, dtype=jnp.int32)[None, :]).astype(jnp.float32)
        coef = (jnp.exp(scores - lse[:, None]) - diagonal).astype(jnp.bfloat16)
        grad_block = jnp.dot(coef, vec, preferred_element_type=jnp.float32) * score_scale
        carry = carry + jnp.dot(coef.T, query_block, preferred_element_type=jnp.float32)
        return (carry, grad_block)
    summed, blocks = lax.scan(step, jnp.zeros((PAIRS, E), jnp.float32), jnp.arange(count, dtype=jnp.int32))
    query_grad = blocks.reshape(PAIRS, E)
    vec_grad = (summed * score_scale).astype(jnp.bfloat16)
    active = (hidden > 0).astype(jnp.float32)
    hidden_grad = (jnp.dot(vec_grad, w_out.T, preferred_element_type=jnp.float32) * active).astype(jnp.bfloat16)
    emb_grad = vec_grad.astype(jnp.float32) + jnp.dot(hidden_grad, w_in.T, preferred_element_type=jnp.float32)
    w_out_grad = jnp.dot(hidden.T, vec_grad, preferred_element_type=jnp.float32)
    w_in_grad = jnp.dot(emb.T, hidden_grad, preferred_element_type=jnp.float32)
    row_grad = jnp.zeros((ROWS, E), jnp.float32).at[item_id].add(emb_grad)
    accum_new = accum + row_grad * row_grad
    table_new = table - learn_rate * row_grad / jnp.sqrt(accum_new)
    return (query_grad, table_new, accum_new, w_in_grad, w_out_grad)
```

```python
import jax
import jax.numpy as jnp
from jax import lax
from jax.experimental import pallas as pl
from jax.experimental.pallas import tpu as pltpu
from jax.sharding import Mesh, PartitionSpec as P

E = 256
H = 512
PAIRS = 192
ROWS = 2048
CAP = 12
SLOT = 16
OWNERS = 32
NA = 16
NB = 8
QS = NA * PAIRS
VS = NB * PAIRS
LIMIT = 40 << 20
score_scale = 0.0625
learn_rate = 0.1

SHARD = ("x", "y", "c")
ALL = ("x", "y", "c", "z")
CHIPS = ("x", "y", "z")
A = ("z", "x")

f32 = jnp.float32
bf16 = jnp.bfloat16
i32 = jnp.int32
VMEM = pltpu.MemorySpace.VMEM
NT = (((1,), (1,)), ((), ()))
TN = (((0,), (0,)), ((), ()))


def mm(a, b, dims=(((1,), (0,)), ((), ()))):
    return lax.dot_general(a, b, dims, preferred_element_type=f32)


def iota(shape, axis):
    return lax.broadcasted_iota(i32, shape, axis)


def call(kernel, out_shape, *, cost=(0, 0, 0), limit=None, **kw):
    return pl.pallas_call(
        kernel,
        out_shape=out_shape,
        compiler_params=pltpu.CompilerParams(vmem_limit_bytes=limit),
        cost_estimate=pl.CostEstimate(flops=cost[0], bytes_accessed=cost[1], transcendentals=cost[2]),
        **kw,
    )


def sds(shape, dtype):
    return jax.ShapeDtypeStruct(shape, dtype)


def column(lanes, rows):
    n = lanes.shape[1]
    eye = iota((rows, n), 0) == iota((rows, n), 1)
    return jnp.sum(jnp.where(eye, lanes, jnp.zeros((), lanes.dtype)), axis=1, keepdims=True)


def slots_kernel(pair_ref, req_ref, place_ref, pick_ref, ids_ref):
    owner = pair_ref[0:1, :]
    row = pair_ref[1:2, :]
    mine = owner == iota((OWNERS, 256), 0)
    onehot = mine.astype(f32).astype(bf16)
    earlier = (iota((256, 256), 0) < iota((256, 256), 1)).astype(f32).astype(bf16)
    before = mm(onehot, earlier)
    slot = jnp.sum(jnp.where(mine, before, 0.0), axis=0, keepdims=True).astype(i32)
    here = slot == iota((128, 256), 0)
    low = jnp.where(here, (row & 255).astype(f32), 0.0).astype(bf16)
    high = jnp.where(here, ((row >> 8) + 1).astype(f32), 0.0).astype(bf16)
    lo = mm(onehot, low, NT)
    hi = mm(onehot, high, NT) - 1.0
    req_ref[...] = jnp.where(hi < 0.0, -1, (hi * 256.0 + lo).astype(i32))
    ids_ref[:, 0:128] = hi
    ids_ref[:, 128:256] = lo
    place = jnp.where(owner < 0, -1, owner * SLOT + slot)
    place_ref[...] = place
    flat = jnp.where(owner < 0, -1, owner * CAP + slot).astype(f32)
    col = column(flat, PAIRS).astype(i32)
    pick_ref[...] = (col == iota((PAIRS, OWNERS * CAP), 1)).astype(f32).astype(bf16)


def tower_kernel(got_ref, pick_ref, w_in_ref, w_out_ref, freq_ref, emb_ref, hid_ref, pay_ref):
    emb = mm(pick_ref[...], got_ref[...]).astype(bf16)
    emb_ref[...] = emb
    hid = jnp.maximum(mm(emb, w_in_ref[...]), 0.0).astype(bf16)
    hid_ref[...] = hid
    vec = (emb.astype(f32) + mm(hid, w_out_ref[...])).astype(bf16)
    pay_ref[0:PAIRS, :] = vec
    pay_ref[PAIRS : PAIRS + 16, :] = freq_ref[...]


QB = 256


def load_vecs(vec_refs, vec, freq):
    for b in range(NB):
        at = slice(b * PAIRS, (b + 1) * PAIRS)
        line = vec_refs[b][PAIRS : PAIRS + 16, :].astype(f32)[0:1, :]
        freq[at, :] = jnp.broadcast_to(column(line, PAIRS), (PAIRS, 128))
        vec[at, :] = vec_refs[b][0:PAIRS, :]


def lanes(col, n):
    return jnp.concatenate([col] * (n // 128), axis=1)


def score_kernel(*refs):
    vec_refs, (q_ref, ml_ref, vec, freq, scores) = refs[:NB], refs[NB:]

    @pl.when(pl.program_id(0) == 0)
    def _():
        load_vecs(vec_refs, vec, freq)

    q = q_ref[...] * jnp.asarray(score_scale, bf16)
    top = None
    for b in range(NB):
        at = slice(b * PAIRS, (b + 1) * PAIRS)
        s = mm(vec[at, :], q, NT) - lanes(freq[at, :], QB)
        scores[at, :] = s
        t = jnp.max(s, axis=0, keepdims=True)
        top = t if top is None else jnp.maximum(top, t)
    total = jnp.zeros((1, QB), f32)
    for b in range(NB):
        at = slice(b * PAIRS, (b + 1) * PAIRS)
        total = total + jnp.sum(jnp.exp(scores[at, :] - top), axis=0, keepdims=True)
    ml_ref[0:1, :] = top
    ml_ref[1:2, :] = total


CB = 384


def grad_kernel(pos_ref, *refs):
    vec_refs, (all_ml_ref, q_ref, o_ref, same_ref, other_ref, vec, freq, turned, lse, coef) = refs[:NB], refs[NB:]
    step = pl.program_id(0)

    @pl.when(step == 0)
    def _():
        load_vecs(vec_refs, vec, freq)
        for k in range(0, VS, 256):
            turned[:, k : k + 256] = vec[k : k + 256, :].astype(f32).T.astype(bf16)
        top = all_ml_ref[0, 0:1, :]
        for a in range(1, NA):
            top = jnp.maximum(top, all_ml_ref[a, 0:1, :])
        total = jnp.zeros((1, QS), f32)
        for a in range(NA):
            total = total + jnp.exp(all_ml_ref[a, 0:1, :] - top) * all_ml_ref[a, 1:2, :]
        whole_lse = top + jnp.log(total)
        for k in range(QS // CB):
            lse[k, :, :] = jnp.broadcast_to(whole_lse[:, k * CB : (k + 1) * CB], (8, CB))
        same_ref[...] = jnp.zeros_like(same_ref)
        other_ref[...] = jnp.zeros_like(other_ref)

    q = q_ref[...]
    scaled = q * jnp.asarray(score_scale, bf16)
    norm = lse[step][0:1, :]
    first = pos_ref[0] * PAIRS - step * CB
    for b in range(NB):
        at = slice(b * PAIRS, (b + 1) * PAIRS)
        p = jnp.exp(mm(vec[at, :], scaled, NT) - lanes(freq[at, :], CB) - norm)
        if b == 0:
            p = jnp.where(iota((PAIRS, CB), 0) + first == iota((PAIRS, CB), 1), p - 1.0, p)
        coef[at, :] = p.astype(bf16)
    o_ref[...] = mm(turned[...], coef[...]).T.astype(bf16)
    for b in range(NB):
        at = slice(b * PAIRS, (b + 1) * PAIRS)
        ref = (same_ref, other_ref)[b // 4]
        ref[b % 4] += mm(coef[at, :], q)


def back_kernel(*refs):
    parts, (emb_ref, hid_ref, w_out_ref, place_ref, ids_ref, out_ref) = refs[:4], refs[4:]
    total = parts[0][...]
    for part in parts[1:]:
        total = total + part[...]
    grad = (total * score_scale).astype(bf16)
    hid = hid_ref[...]
    hg = jnp.where(hid.astype(f32) > 0.0, mm(grad, w_out_ref[...], NT), 0.0).astype(bf16)
    scatter = (iota((OWNERS * SLOT, PAIRS), 0) == place_ref[:, 0:PAIRS]).astype(f32).astype(bf16)
    slots = mm(scatter, grad).reshape(OWNERS, SLOT, E)
    ids = ids_ref[...].reshape(OWNERS, 1, E)
    slots = jnp.where(iota((OWNERS, SLOT, E), 1) == CAP, ids, slots).astype(bf16).reshape(16, 2, SLOT, E)
    w_out_part = mm(hid, grad, TN)
    w_in_part = mm(emb_ref[...], hg, TN)
    pieces = []
    for part in (w_out_part, w_in_part):
        n = part.shape[0] // 8
        tiles = [part[:, k : k + 128].reshape(n, 1, 8, 128) for k in range(0, part.shape[1], 128)]
        pieces.append(jnp.concatenate(tiles, axis=1).reshape(16, 4, SLOT, 128).astype(bf16))
    for z in range(4):
        out_ref[:, :, z, :, 0:E] = slots
        for c in range(2):
            out_ref[:, c, z, :, E : E + 128] = pieces[c][:, z]


TB = 256


def update_kernel(ids_ref, got_ref, table_ref, accum_ref, w_in_ref, w_out_ref, table_out, accum_out):
    base = pl.program_id(0) * TB
    onehot = (ids_ref[...] == iota((TB, 128 * SLOT), 0) + base).astype(f32).astype(bf16)
    vals = got_ref[:, :, 0:E].reshape(128 * SLOT, E)
    vg = mm(onehot, vals)
    high = vg.astype(bf16)
    low = (vg - high.astype(f32)).astype(bf16)
    table = table_ref[...]
    hid = jnp.maximum(mm(table.astype(bf16), w_in_ref[...]), 0.0).astype(bf16).astype(f32)
    back = mm(high, w_out_ref[...], NT) + mm(low, w_out_ref[...], NT)
    hg = jnp.where(hid > 0.0, back, 0.0).astype(bf16)
    g = vg + mm(hg, w_in_ref[...], NT)
    acc = accum_ref[...] + g * g
    accum_out[...] = acc
    table_out[...] = table - learn_rate * g / jnp.sqrt(acc)


def a2a(x, axes):
    return lax.all_to_all(x, axes, split_axis=0, concat_axis=0, tiled=True)


def shift(x, axis, k):
    n = 2 if axis == "c" else 4
    return lax.ppermute(x, axis, [(i, (i + k) % n) for i in range(n)])


def whole(n):
    return [pl.BlockSpec(memory_space=VMEM)] * n


def const(*shape):
    return pl.BlockSpec(shape, lambda *_: (0,) * len(shape))


def local(queries, item_owner, item_row, log_freq, table, accum, w_in, w_out):
    all_q = lax.all_gather(queries, A, axis=0, tiled=True)
    here = lax.axis_index(A).astype(i32)
    here_x = lax.axis_index("x").astype(i32)
    here_z = lax.axis_index("z").astype(i32)

    pair = jnp.stack(
        [
            jnp.pad(item_owner[:, 0], (0, 256 - PAIRS), constant_values=-1),
            jnp.pad(item_row, (0, 256 - PAIRS)),
        ]
    )
    req, place, pick, ids = call(
        slots_kernel,
        (
            sds((OWNERS, 128), i32),
            sds((1, 256), i32),
            sds((PAIRS, OWNERS * CAP), bf16),
            sds((OWNERS, E), f32),
        ),
        in_specs=whole(1),
        out_specs=tuple(whole(4)),
    )(pair)
    asked = a2a(req.reshape(OWNERS, 1, 128), SHARD)
    wanted = jnp.maximum(asked[:, 0, :CAP].reshape(OWNERS * CAP), 0)
    picked = table.at[wanted].get(mode="promise_in_bounds").astype(bf16)
    got = a2a(picked.reshape(OWNERS, CAP, E), SHARD).reshape(OWNERS * CAP, E)
    freq_row = jnp.pad(log_freq.reshape(1, PAIRS), ((0, 15), (0, 256 - PAIRS)))
    emb, hid, pay = call(
        tower_kernel,
        (sds((PAIRS, E), bf16), sds((PAIRS, H), bf16), sds((PAIRS + 16, E), bf16)),
        in_specs=whole(5),
        out_specs=tuple(whole(3)),
    )(got, pick, w_in, w_out, freq_row)
    vecs = [pay] + [shift(pay, "y", k) for k in range(1, 4)]
    vecs = vecs + [shift(v, "c", 1) for v in vecs]

    ml = call(
        score_kernel,
        sds((2, QS), f32),
        cost=(2 * VS * QS * E, VS * QS * 2, VS * QS),
        limit=LIMIT,
        grid=(QS // QB,),
        in_specs=[const(PAIRS + 16, E)] * NB + [pl.BlockSpec((QB, E), lambda i: (i, 0))],
        out_specs=pl.BlockSpec((2, QB), lambda i: (0, i)),
        scratch_shapes=[pltpu.VMEM((VS, E), bf16), pltpu.VMEM((VS, 128), f32), pltpu.VMEM((VS, QB), f32)],
    )(*vecs, all_q)
    all_ml = a2a(jnp.broadcast_to(ml[None], (NA, 2, QS)), A)

    per = QS // 4 // CB
    o, same, other = call(
        grad_kernel,
        (sds((QS, E), bf16), sds((4, PAIRS, E), f32), sds((4, PAIRS, E), f32)),
        cost=(6 * VS * QS * E, VS * QS * 2, VS * QS),
        limit=LIMIT,
        grid_spec=pltpu.PrefetchScalarGridSpec(
            num_scalar_prefetch=1,
            grid=(QS // CB,),
            in_specs=[const(PAIRS + 16, E)] * NB
            + [const(NA, 2, QS), pl.BlockSpec((CB, E), lambda i, pos: (i, 0))],
            out_specs=(
                pl.BlockSpec((CB, E), lambda i, pos: (((i // per - pos[1] + 4) % 4) * per + i % per, 0)),
                const(4, PAIRS, E),
                const(4, PAIRS, E),
            ),
            scratch_shapes=[
                pltpu.VMEM((VS, E), bf16),
                pltpu.VMEM((VS, 128), f32),
                pltpu.VMEM((E, VS), bf16),
                pltpu.VMEM((QS // CB, 8, CB), f32),
                pltpu.VMEM((VS, CB), bf16),
            ],
        ),
    )(jnp.stack([here, here_z]), *vecs, all_ml, all_q)

    from_core = shift(other, "c", 1)
    sums = [same[k] + from_core[k] for k in range(4)]
    parts = [sums[0]] + [shift(sums[k], "y", 4 - k) for k in range(1, 4)]
    out = call(
        back_kernel,
        sds((16, 2, 4, SLOT, E + 128), bf16),
        limit=LIMIT,
        in_specs=whole(9),
        out_specs=whole(1)[0],
    )(*parts, emb, hid, w_out, place, ids)
    back = a2a(out.reshape(128, SLOT, E + 128), ALL)

    slab = QS // 4
    slabs = [o[:slab]] + [shift(o[k * slab : (k + 1) * slab], "z", k) for k in range(1, 4)]

    def toward(k):
        at = ((here_x + k) % 4) * PAIRS
        return sum(lax.dynamic_slice(v, (at, 0), (PAIRS, E)).astype(f32) for v in slabs)

    query_grad = toward(0)
    for k in range(1, 4):
        query_grad = query_grad + shift(toward(k), "x", k)
    query_grad = query_grad * score_scale

    w_sum = jnp.sum(back[:, :, E:].astype(f32), axis=0)
    w_mine = a2a(jnp.broadcast_to(w_sum[None], (64, SLOT, 128)), CHIPS)
    w_other = shift(w_mine, "c", 1)
    zero = lax.axis_index("c") == 0

    def tiles(x, rows, cols):
        return x.reshape(rows // 8, cols // 128, 8, 128).transpose(0, 2, 1, 3).reshape(rows, cols)

    w_out_grad = tiles(jnp.where(zero, w_mine, w_other), H, E)
    w_in_grad = tiles(jnp.where(zero, w_other, w_mine), E, H)

    hi = back[:, CAP, 0:CAP].astype(i32)
    lo = back[:, CAP, 128 : 128 + CAP].astype(i32)
    row_ids = jnp.where(hi < 0, -1, hi * 256 + lo)
    row_ids = jnp.pad(row_ids, ((0, 0), (0, SLOT - CAP)), constant_values=-1).reshape(1, 128 * SLOT)
    table_new, accum_new = call(
        update_kernel,
        (sds((ROWS, E), f32), sds((ROWS, E), f32)),
        cost=(4 * ROWS * 2048 * E, 4 * ROWS * E * 4, 0),
        limit=LIMIT,
        grid=(ROWS // TB,),
        in_specs=[
            const(1, 128 * SLOT),
            const(128, SLOT, E + 128),
            pl.BlockSpec((TB, E), lambda i: (i, 0)),
            pl.BlockSpec((TB, E), lambda i: (i, 0)),
            const(E, H),
            const(H, E),
        ],
        out_specs=(
            pl.BlockSpec((TB, E), lambda i: (i, 0)),
            pl.BlockSpec((TB, E), lambda i: (i, 0)),
        ),
    )(row_ids, back, table, accum, w_in, w_out)
    return query_grad, table_new, accum_new, w_in_grad, w_out_grad


def solution(mesh):
    fine = Mesh(mesh.devices.reshape(4, 4, 2, 4), ALL)
    return jax.shard_map(
        local,
        mesh=fine,
        in_specs=(
            P(ALL, None),
            P(ALL, None),
            P(ALL),
            P(ALL),
            P(SHARD, None),
            P(SHARD, None),
            P(),
            P(),
        ),
        out_specs=(P(ALL, None), P(SHARD, None), P(SHARD, None), P(), P()),
        check_vma=False,
    )
```

```python
import jax
import jax.numpy as jnp
from jax import lax
from jax.experimental import pallas as pl
from jax.experimental.pallas import tpu as pltpu
from jax.sharding import Mesh, PartitionSpec as P

E = 256
H = 512
PAIRS = 192
ROWS = 2048
CAP = 12
SLOT = 16
OWNERS = 32
NA = 16
NB = 8
QS = NA * PAIRS
VS = NB * PAIRS
LIMIT = 58 << 20
SMALL = 24 << 20
score_scale = 0.0625
learn_rate = 0.1

SHARD = ("x", "y", "c")
ALL = ("x", "y", "c", "z")
CHIPS = ("x", "y", "z")
A = ("x", "z")

f32 = jnp.float32
bf16 = jnp.bfloat16
i32 = jnp.int32
VMEM = pltpu.MemorySpace.VMEM
NT = (((1,), (1,)), ((), ()))
TN = (((0,), (0,)), ((), ()))


def mm(a, b, dims=(((1,), (0,)), ((), ()))):
    return lax.dot_general(a, b, dims, preferred_element_type=f32)


def iota(shape, axis):
    return lax.broadcasted_iota(i32, shape, axis)


def call(kernel, out_shape, *, cost=(0, 0, 0), limit=None, **kw):
    return pl.pallas_call(
        kernel,
        out_shape=out_shape,
        compiler_params=pltpu.CompilerParams(vmem_limit_bytes=limit),
        cost_estimate=pl.CostEstimate(flops=cost[0], bytes_accessed=cost[1], transcendentals=cost[2]),
        **kw,
    )


def sds(shape, dtype):
    return jax.ShapeDtypeStruct(shape, dtype)


def column(lanes, rows):
    n = lanes.shape[1]
    eye = iota((rows, n), 0) == iota((rows, n), 1)
    return jnp.sum(jnp.where(eye, lanes, jnp.zeros((), lanes.dtype)), axis=1, keepdims=True)


def slots_kernel(owner_ref, row_ref, req_ref, place_ref, pick_ref, ids_ref, pair):
    pair[...] = jnp.full((8, 256), -1, i32)
    pair[0:1, 0:PAIRS] = owner_ref[...]
    pair[1:2, 0:PAIRS] = row_ref[...]
    owner = pair[0:1, :]
    row = pair[1:2, :]
    mine = owner == iota((OWNERS, 256), 0)
    onehot = mine.astype(f32).astype(bf16)
    earlier = (iota((256, 256), 0) < iota((256, 256), 1)).astype(f32).astype(bf16)
    before = mm(onehot, earlier)
    slot = jnp.sum(jnp.where(mine, before, 0.0), axis=0, keepdims=True).astype(i32)
    here = slot == iota((128, 256), 0)
    low = jnp.where(here, (row & 255).astype(f32), 0.0).astype(bf16)
    high = jnp.where(here, ((row >> 8) + 1).astype(f32), 0.0).astype(bf16)
    lo = mm(onehot, low, NT)
    hi = mm(onehot, high, NT) - 1.0
    req_ref[...] = jnp.where(hi < 0.0, -1, (hi * 256.0 + lo).astype(i32))
    ids_ref[:, 0:128] = hi
    ids_ref[:, 128:256] = lo
    place = jnp.where(owner < 0, -1, owner * SLOT + slot)
    place_ref[...] = place
    flat = jnp.where(owner < 0, -1, owner * CAP + slot).astype(f32)
    col = column(flat, PAIRS).astype(i32)
    pick_ref[...] = (col == iota((PAIRS, OWNERS * CAP), 1)).astype(f32).astype(bf16)


def tower_kernel(got_ref, pick_ref, w_in_ref, w_out_ref, freq_ref, *refs):
    emb_ref, hid_ref, pay_ref = refs[-3:]
    emb = mm(pick_ref[...], got_ref[...]).astype(bf16)
    emb_ref[...] = emb
    hid = jnp.maximum(mm(emb, w_in_ref[...]), 0.0).astype(bf16)
    hid_ref[...] = hid
    vec = (emb.astype(f32) + mm(hid, w_out_ref[...])).astype(bf16)
    pay_ref[0:PAIRS, :] = vec
    pay_ref[PAIRS : PAIRS + 16, :] = freq_ref[...]


QB = 768
VB = 384


def load_vecs(vec_refs, vec, freq):
    for b in range(NB):
        at = slice(b * PAIRS, (b + 1) * PAIRS)
        line = vec_refs[b][PAIRS : PAIRS + 16, :].astype(f32)[0:1, :]
        freq[at, :] = jnp.broadcast_to(column(line, PAIRS), (PAIRS, 128))
        vec[at, :] = vec_refs[b][0:PAIRS, :]


def lanes(col):
    return jnp.concatenate([col] * (QB // 128), axis=1)


def score_kernel(*refs):
    vec_refs, (q_ref, lse_ref, vec, freq, scores) = refs[:NB], refs[NB:]

    @pl.when(pl.program_id(0) == 0)
    def _():
        load_vecs(vec_refs, vec, freq)

    q = q_ref[...] * jnp.asarray(score_scale, bf16)
    top = None
    for b in range(0, VS, VB):
        at = slice(b, b + VB)
        s = mm(vec[at, :], q, NT) - lanes(freq[at, :])
        scores[at, :] = s
        t = jnp.max(s.reshape(VB // 8, 8, QB), axis=0)
        top = t if top is None else jnp.maximum(top, t)
    top = jnp.max(top, axis=0, keepdims=True)
    total = jnp.zeros((8, QB), f32)
    for b in range(0, VS, VB):
        e = jnp.exp(scores[b : b + VB, :] - top)
        total = total + jnp.sum(e.reshape(VB // 8, 8, QB), axis=0)
    part = top + jnp.log(jnp.sum(total, axis=0, keepdims=True))
    for k in range(QB // 128):
        row = jnp.broadcast_to(part[:, k * 128 : (k + 1) * 128].reshape(1, 1, 128), (NA, 1, 128))
        lse_ref[:, pl.ds(pl.program_id(0) * (QB // 128) + k, 1), :] = row


def is_pair(pos_ref):
    first = pos_ref[0] * PAIRS - pl.program_id(0) * QB
    return iota((PAIRS, QB), 0) + first == iota((PAIRS, QB), 1)


def query_lanes(rows_ref, *index):
    n = QB // 128
    at = pl.program_id(0) * n
    return jnp.concatenate([rows_ref[(*index, pl.ds(at + i, 1), slice(None))] for i in range(n)], axis=1)


def query_kernel(pos_ref, *refs):
    vec_refs, (part_ref, q_ref, o_ref, vec, freq, turned, weight) = refs[:NB], refs[NB:]

    @pl.when(pl.program_id(0) == 0)
    def _():
        load_vecs(vec_refs, vec, freq)
        for k in range(0, VS, 256):
            turned[:, k : k + 256] = vec[k : k + 256, :].astype(f32).T.astype(bf16)

    q = q_ref[...] * jnp.asarray(score_scale, bf16)
    norm = query_lanes(part_ref, 0).reshape(1, QB)
    for b in range(0, VS, VB):
        at = slice(b, b + VB)
        p = jnp.exp(mm(vec[at, :], q, NT) - lanes(freq[at, :]) - norm)
        if b == 0:
            p = jnp.concatenate([jnp.where(is_pair(pos_ref), 0.0, p[:PAIRS]), p[PAIRS:]], axis=0)
        weight[at, :] = p.astype(bf16)
    o_ref[...] = mm(turned[...], weight[...]).T.astype(bf16)


def vec_kernel(pos_ref, vec, freq, parts_ref, q_ref, unread_ref, same_ref, other_ref, lse, coef):
    @pl.when(pl.program_id(0) == 0)
    def _():
        top = parts_ref[0]
        for a in range(1, NA):
            top = jnp.maximum(top, parts_ref[a])
        total = jnp.exp(parts_ref[0] - top)
        for a in range(1, NA):
            total = total + jnp.exp(parts_ref[a] - top)
        lse[...] = top + jnp.log(total)
        same_ref[...] = jnp.zeros_like(same_ref)
        other_ref[...] = jnp.zeros_like(other_ref)

    q = q_ref[...]
    scaled = q * jnp.asarray(score_scale, bf16)
    norm = query_lanes(lse)
    for b in range(0, VS, VB):
        at = slice(b, b + VB)
        p = jnp.exp(mm(vec[at, :], scaled, NT) - lanes(freq[at, :]) - norm)
        if b == 0:
            p = jnp.concatenate([jnp.where(is_pair(pos_ref), p[:PAIRS] - 1.0, p[:PAIRS]), p[PAIRS:]], axis=0)
        coef[at, :] = p.astype(bf16)
    for b in range(0, NB, 2):
        g = mm(coef[b * PAIRS : (b + 2) * PAIRS, :], q)
        ref = (same_ref, other_ref)[b // 4]
        ref[b % 4] += g[:PAIRS]
        ref[b % 4 + 1] += g[PAIRS:]


def combine_kernel(got_ref, parts_ref, q_ref, pay_ref, out_ref):
    parts = parts_ref[...]
    top = jnp.max(parts, axis=0, keepdims=True)
    lse = top + jnp.log(jnp.sum(jnp.exp(parts - top), axis=0, keepdims=True))
    shares = jnp.exp(parts - lse)
    q = q_ref[...].astype(f32)
    vec = pay_ref[0:PAIRS, :].astype(f32)
    line = pay_ref[PAIRS : PAIRS + 16, :].astype(f32)[0:1, :]
    own = jnp.sum(q * vec, axis=1, keepdims=True) * score_scale - column(line, PAIRS) - column(lse, PAIRS)
    total = (jnp.exp(own) - 1.0).astype(bf16).astype(f32) * vec
    for a in range(NA):
        total = total + got_ref[a].astype(f32) * column(shares[a : a + 1], PAIRS)
    out_ref[...] = total * score_scale


def back_kernel(*refs):
    parts, (emb_ref, hid_ref, w_out_ref, place_ref, ids_ref), out_ref = refs[:4], refs[4:9], refs[-1]
    total = parts[0][...]
    for part in parts[1:]:
        total = total + part[...]
    grad = (total * score_scale).astype(bf16)
    hid = hid_ref[...]
    hg = jnp.where(hid.astype(f32) > 0.0, mm(grad, w_out_ref[...], NT), 0.0).astype(bf16)
    scatter = (iota((OWNERS * SLOT, PAIRS), 0) == place_ref[:, 0:PAIRS]).astype(f32).astype(bf16)
    slots = mm(scatter, grad).reshape(OWNERS, SLOT, E)
    ids = ids_ref[...].reshape(OWNERS, 1, E)
    slots = jnp.where(iota((OWNERS, SLOT, E), 1) == CAP, ids, slots).astype(bf16).reshape(16, 2, SLOT, E)
    w_out_part = mm(hid, grad, TN)
    w_in_part = mm(emb_ref[...], hg, TN)
    pieces = []
    for part in (w_out_part, w_in_part):
        n = part.shape[0] // 8
        tiles = [part[:, k : k + 128].reshape(n, 1, 8, 128) for k in range(0, part.shape[1], 128)]
        pieces.append(jnp.concatenate(tiles, axis=1).reshape(16, 4, SLOT, 128).astype(bf16))
    for z in range(4):
        out_ref[:, :, z, :, 0:E] = slots
        for c in range(2):
            out_ref[:, c, z, :, E : E + 128] = pieces[c][:, z]


TB = 512


def update_kernel(ids_ref, got_ref, table_ref, accum_ref, w_in_ref, w_out_ref, table_out, accum_out):
    base = pl.program_id(0) * TB
    onehot = (ids_ref[...] == iota((TB, 128 * SLOT), 0) + base).astype(f32).astype(bf16)
    vals = got_ref[:, :, 0:E].reshape(128 * SLOT, E)
    vg = mm(onehot, vals)
    high = vg.astype(bf16)
    low = (vg - high.astype(f32)).astype(bf16)
    table = table_ref[...]
    hid = jnp.maximum(mm(table.astype(bf16), w_in_ref[...]), 0.0).astype(bf16).astype(f32)
    back = mm(high, w_out_ref[...], NT) + mm(low, w_out_ref[...], NT)
    hg = jnp.where(hid > 0.0, back, 0.0).astype(bf16)
    g = vg + mm(hg, w_in_ref[...], NT)
    acc = accum_ref[...] + g * g
    accum_out[...] = acc
    table_out[...] = table - learn_rate * g / jnp.sqrt(acc)


def a2a(x, axes):
    return lax.all_to_all(x, axes, split_axis=0, concat_axis=0, tiled=True)


def shift(x, axis, k):
    n = 2 if axis == "c" else 4
    return lax.ppermute(x, axis, [(i, (i + k) % n) for i in range(n)])


def whole(n):
    return [pl.BlockSpec(memory_space=VMEM)] * n


def unread(n):
    return [pl.BlockSpec(memory_space=pl.ANY)] * n


def after(x, *others):
    return pl.pallas_call(
        lambda *refs: None,
        out_shape=sds(x.shape, x.dtype),
        in_specs=unread(1 + len(others)),
        out_specs=unread(1)[0],
        input_output_aliases={0: 0},
    )(x, *others)


def const(*shape):
    return pl.BlockSpec(shape, lambda *_: (0,) * len(shape))


def local(queries, item_owner, item_row, log_freq, table, accum, w_in, w_out):
    here_x = lax.axis_index("x").astype(i32)
    here_z = lax.axis_index("z").astype(i32)
    req, place, pick, ids = call(
        slots_kernel,
        (
            sds((OWNERS, 128), i32),
            sds((1, 256), i32),
            sds((PAIRS, OWNERS * CAP), bf16),
            sds((OWNERS, E), f32),
        ),
        in_specs=whole(2),
        out_specs=tuple(whole(4)),
        scratch_shapes=[pltpu.VMEM((8, 256), i32)],
    )(item_owner.reshape(1, PAIRS), item_row.reshape(1, PAIRS))
    asked = a2a(req.reshape(OWNERS, 1, 128), SHARD)
    early = after(queries, req)
    slab = jnp.zeros((QB, E), bf16)
    for k in range(4):
        block = shift(early, "z", 4 - k) if k else queries
        slab = lax.dynamic_update_slice(slab, block, ((here_z + k) % 4 * PAIRS, 0))
    slabs = [slab] + [shift(slab, "x", 4 - k) for k in range(1, 4)]
    all_q = jnp.zeros((QS, E), bf16)
    for k in range(4):
        all_q = lax.dynamic_update_slice(all_q, slabs[k], ((here_x + k) % 4 * QB, 0))
    wanted = jnp.maximum(asked[:, 0, :CAP].reshape(OWNERS * CAP), 0)
    picked = table.at[wanted].get(mode="promise_in_bounds").astype(bf16)
    got = a2a(picked.reshape(OWNERS, CAP, E), SHARD).reshape(OWNERS * CAP, E)
    freq_row = jnp.pad(log_freq.reshape(1, PAIRS), ((0, 15), (0, 256 - PAIRS)))
    emb, hid, pay = call(
        tower_kernel,
        (sds((PAIRS, E), bf16), sds((PAIRS, H), bf16), sds((PAIRS + 16, E), bf16)),
        in_specs=whole(5) + unread(2),
        out_specs=tuple(whole(3)),
    )(got, pick, w_in, w_out, freq_row, slabs[1], slabs[3])
    vecs = [pay] + [shift(pay, "y", k) for k in range(1, 4)]
    vecs = vecs + [shift(v, "c", 1) for v in vecs]

    part_lse = call(
        score_kernel,
        sds((NA, QS // 128, 128), f32),
        cost=(2 * VS * QS * E, VS * QS * 2, VS * QS),
        limit=LIMIT,
        grid=(QS // QB,),
        in_specs=[const(PAIRS + 16, E)] * NB + [pl.BlockSpec((QB, E), lambda i: (i, 0))],
        out_specs=const(NA, QS // 128, 128),
        scratch_shapes=[pltpu.VMEM((VS, E), bf16), pltpu.VMEM((VS, 128), f32), pltpu.VMEM((VS, QB), f32)],
    )(*vecs, all_q)
    all_lse = a2a(part_lse, A)
    here = here_x * 4 + here_z
    o, vec_all, freq_all = call(
        query_kernel,
        (sds((QS, E), bf16), sds((VS, E), bf16), sds((VS, 128), f32)),
        cost=(4 * VS * QS * E, VS * QS, VS * QS),
        limit=LIMIT,
        grid_spec=pltpu.PrefetchScalarGridSpec(
            num_scalar_prefetch=1,
            grid=(QS // QB,),
            in_specs=[const(PAIRS + 16, E)] * NB
            + [const(NA, QS // 128, 128), pl.BlockSpec((QB, E), lambda i, pos: (i, 0))],
            out_specs=(pl.BlockSpec((QB, E), lambda i, pos: (i, 0)), const(VS, E), const(VS, 128)),
            scratch_shapes=[pltpu.VMEM((E, VS), bf16), pltpu.VMEM((VS, QB), bf16)],
        ),
    )(here.reshape(1), *vecs, part_lse, all_q)
    same, other = call(
        vec_kernel,
        (sds((4, PAIRS, E), f32), sds((4, PAIRS, E), f32)),
        cost=(4 * VS * QS * E, VS * QS, VS * QS),
        limit=LIMIT,
        grid_spec=pltpu.PrefetchScalarGridSpec(
            num_scalar_prefetch=1,
            grid=(QS // QB,),
            in_specs=[
                const(VS, E),
                const(VS, 128),
                const(NA, QS // 128, 128),
                pl.BlockSpec((QB, E), lambda i, pos: (i, 0)),
                unread(1)[0],
            ],
            out_specs=(const(4, PAIRS, E), const(4, PAIRS, E)),
            scratch_shapes=[pltpu.VMEM((QS // 128, 128), f32), pltpu.VMEM((VS, QB), bf16)],
        ),
    )(here.reshape(1), vec_all, freq_all, all_lse, all_q, o)
    o_got = a2a(o.reshape(NA, PAIRS, E), A)

    from_core = shift(other, "c", 1)
    sums = [same[k] + from_core[k] for k in range(4)]
    parts = [sums[0]] + [shift(sums[k], "y", 4 - k) for k in range(1, 4)]
    out = call(
        back_kernel,
        sds((16, 2, 4, SLOT, E + 128), bf16),
        limit=SMALL,
        in_specs=whole(9) + unread(1),
        out_specs=whole(1)[0],
    )(*parts, emb, hid, w_out, place, ids, o_got)
    back = a2a(out.reshape(128, SLOT, E + 128), ALL)

    own = lax.dynamic_slice(all_lse.reshape(NA, QS), (0, here * PAIRS), (NA, PAIRS))
    query_grad = call(
        combine_kernel,
        sds((PAIRS, E), f32),
        limit=SMALL,
        in_specs=whole(4),
        out_specs=whole(1)[0],
    )(o_got, jnp.pad(own, ((0, 0), (0, 256 - PAIRS))), queries, pay)

    w_sum = jnp.sum(back[:, :, E:].astype(f32), axis=0)
    w_mine = a2a(jnp.broadcast_to(w_sum[None], (64, SLOT, 128)), CHIPS)
    hi = back[:, CAP, 0:CAP].astype(i32)
    lo = back[:, CAP, 128 : 128 + CAP].astype(i32)
    row_ids = jnp.where(hi < 0, -1, hi * 256 + lo)
    row_ids = jnp.pad(row_ids, ((0, 0), (0, SLOT - CAP)), constant_values=-1).reshape(1, 128 * SLOT)
    table_new, accum_new = call(
        update_kernel,
        (sds((ROWS, E), f32), sds((ROWS, E), f32)),
        cost=(4 * ROWS * 2048 * E, 4 * ROWS * E * 4, 0),
        limit=LIMIT,
        grid=(ROWS // TB,),
        in_specs=[
            const(1, 128 * SLOT),
            const(128, SLOT, E + 128),
            pl.BlockSpec((TB, E), lambda i: (i, 0)),
            pl.BlockSpec((TB, E), lambda i: (i, 0)),
            const(E, H),
            const(H, E),
        ],
        out_specs=(
            pl.BlockSpec((TB, E), lambda i: (i, 0)),
            pl.BlockSpec((TB, E), lambda i: (i, 0)),
        ),
    )(row_ids, back, table, accum, w_in, w_out)
    w_mine = after(w_mine, table_new)
    w_other = shift(w_mine, "c", 1)
    zero = lax.axis_index("c") == 0

    def tiles(x, rows, cols):
        return x.reshape(rows // 8, cols // 128, 8, 128).transpose(0, 2, 1, 3).reshape(rows, cols)

    w_out_grad = tiles(jnp.where(zero, w_mine, w_other), H, E)
    w_in_grad = tiles(jnp.where(zero, w_other, w_mine), E, H)

    return query_grad, table_new, accum_new, w_in_grad, w_out_grad


def solution(mesh):
    fine = Mesh(mesh.devices.reshape(4, 4, 2, 4), ALL)
    return jax.shard_map(
        local,
        mesh=fine,
        in_specs=(
            P(ALL, None),
            P(ALL, None),
            P(ALL),
            P(ALL),
            P(SHARD, None),
            P(SHARD, None),
            P(),
            P(),
        ),
        out_specs=(P(ALL, None), P(SHARD, None), P(SHARD, None), P(), P()),
        check_vma=False,
    )
```

```python
import jax
import jax.numpy as jnp
from jax import lax
from jax.experimental import pallas as pl
from jax.experimental.pallas import tpu as pltpu
from jax.sharding import Mesh, PartitionSpec as P

E = 256
H = 512
PAIRS = 192
ROWS = 2048
CAP = 12
SLOT = 16
OWNERS = 32
NA = 16
NB = 8
QS = NA * PAIRS
VS = NB * PAIRS
LIMIT = 58 << 20
SMALL = 24 << 20
score_scale = 0.0625
learn_rate = 0.1

SHARD = ("x", "y", "c")
ALL = ("x", "y", "c", "z")
A = ("z", "x")

f32 = jnp.float32
bf16 = jnp.bfloat16
i32 = jnp.int32
VMEM = pltpu.MemorySpace.VMEM
NT = (((1,), (1,)), ((), ()))
TN = (((0,), (0,)), ((), ()))


def mm(a, b, dims=(((1,), (0,)), ((), ()))):
    return lax.dot_general(a, b, dims, preferred_element_type=f32)


def iota(shape, axis):
    return lax.broadcasted_iota(i32, shape, axis)


def call(kernel, out_shape, *, cost=(0, 0, 0), limit=None, **kw):
    return pl.pallas_call(
        kernel,
        out_shape=out_shape,
        compiler_params=pltpu.CompilerParams(vmem_limit_bytes=limit),
        cost_estimate=pl.CostEstimate(flops=cost[0], bytes_accessed=cost[1], transcendentals=cost[2]),
        **kw,
    )


def sds(shape, dtype):
    return jax.ShapeDtypeStruct(shape, dtype)


def column(lanes, rows):
    n = lanes.shape[1]
    eye = iota((rows, n), 0) == iota((rows, n), 1)
    return jnp.sum(jnp.where(eye, lanes, jnp.zeros((), lanes.dtype)), axis=1, keepdims=True)


def slots_kernel(owner_ref, row_ref, req_ref, place_ref, pick_ref, ids_ref, pair):
    pair[...] = jnp.full((8, 256), -1, i32)
    pair[0:1, 0:PAIRS] = owner_ref[...]
    pair[1:2, 0:PAIRS] = row_ref[...]
    owner = pair[0:1, :]
    row = pair[1:2, :]
    mine = owner == iota((OWNERS, 256), 0)
    onehot = mine.astype(f32).astype(bf16)
    earlier = (iota((256, 256), 0) < iota((256, 256), 1)).astype(f32).astype(bf16)
    before = mm(onehot, earlier)
    slot = jnp.sum(jnp.where(mine, before, 0.0), axis=0, keepdims=True).astype(i32)
    here = slot == iota((128, 256), 0)
    low = jnp.where(here, (row & 255).astype(f32), 0.0).astype(bf16)
    high = jnp.where(here, ((row >> 8) + 1).astype(f32), 0.0).astype(bf16)
    lo = mm(onehot, low, NT)
    hi = mm(onehot, high, NT) - 1.0
    req_ref[...] = jnp.where(hi < 0.0, -1, (hi * 256.0 + lo).astype(i32))
    ids_ref[:, 0:128] = hi
    ids_ref[:, 128:256] = lo
    place = jnp.where(owner < 0, -1, owner * SLOT + slot)
    place_ref[...] = place
    flat = jnp.where(owner < 0, -1, owner * CAP + slot).astype(f32)
    col = column(flat, PAIRS).astype(i32)
    pick_ref[...] = (col == iota((PAIRS, OWNERS * CAP), 1)).astype(f32).astype(bf16)


def tower_kernel(got_ref, pick_ref, w_in_ref, w_out_ref, freq_ref, *refs):
    emb_ref, hid_ref, pay_ref = refs[-3:]
    emb = mm(pick_ref[...], got_ref[...]).astype(bf16)
    emb_ref[...] = emb
    hid = jnp.maximum(mm(emb, w_in_ref[...]), 0.0).astype(bf16)
    hid_ref[...] = hid
    vec = (emb.astype(f32) + mm(hid, w_out_ref[...])).astype(bf16)
    pay_ref[0:PAIRS, :] = vec
    pay_ref[PAIRS : PAIRS + 16, :] = freq_ref[...]


QB = 768
VB = 384


def load_vecs(vec_refs, vec, freq):
    for b in range(NB):
        at = slice(b * PAIRS, (b + 1) * PAIRS)
        line = vec_refs[b][PAIRS : PAIRS + 16, :].astype(f32)[0:1, :]
        freq[at, :] = jnp.broadcast_to(column(line, PAIRS), (PAIRS, 128))
        vec[at, :] = vec_refs[b][0:PAIRS, :]


def lanes(col, n=QB):
    return jnp.concatenate([col] * (n // 128), axis=1)


PB = 512


def score_kernel(*refs):
    vec_refs, (q_ref, lse_ref, vec, freq, *scores) = refs[:NB], refs[NB:]
    load_vecs(vec_refs, vec, freq)
    tops = []
    for j in range(QS // PB + 1):
        top, total = None, jnp.zeros((8, PB), f32)
        if j < QS // PB:
            q = q_ref[j * PB : (j + 1) * PB, :] * jnp.asarray(score_scale, bf16)
        for b in range(0, VS, VB):
            at = slice(b, b + VB)
            if j < QS // PB:
                s = mm(vec[at, :], q, NT) - lanes(freq[at, :], PB)
                scores[j % 2][at, :] = s
                t = jnp.max(s.reshape(VB // 8, 8, PB), axis=0)
                top = t if top is None else jnp.maximum(top, t)
            if j > 0:
                e = jnp.exp(scores[(j - 1) % 2][at, :] - tops[j - 1])
                total = total + jnp.sum(e.reshape(VB // 8, 8, PB), axis=0)
        if j < QS // PB:
            tops.append(jnp.max(top, axis=0, keepdims=True))
        if j > 0:
            part = tops[j - 1] + jnp.log(jnp.sum(total, axis=0, keepdims=True))
            n = PB // 128
            for k in range(n):
                row = part[:, k * 128 : (k + 1) * 128].reshape(1, 1, 128)
                at = (j - 1) * n + k
                lse_ref[:, at : at + 1, :] = jnp.broadcast_to(row, (NA, 1, 128))


def is_pair(pos_ref):
    first = pos_ref[0] * PAIRS - pl.program_id(0) * QB
    return iota((PAIRS, QB), 0) + first == iota((PAIRS, QB), 1)


def query_lanes(rows_ref, *index):
    n = QB // 128
    at = pl.program_id(0) * n
    return jnp.concatenate([rows_ref[(*index, pl.ds(at + i, 1), slice(None))] for i in range(n)], axis=1)


def query_kernel(pos_ref, *refs):
    vec_refs, (part_ref, q_ref, o_ref, vec, freq, turned, weight) = refs[:NB], refs[NB:]

    @pl.when(pl.program_id(0) == 0)
    def _():
        load_vecs(vec_refs, vec, freq)
        for k in range(0, VS, 256):
            turned[:, k : k + 256] = vec[k : k + 256, :].astype(f32).T.astype(bf16)

    q = q_ref[...] * jnp.asarray(score_scale, bf16)
    norm = query_lanes(part_ref, 0).reshape(1, QB)
    for b in range(0, VS, VB):
        at = slice(b, b + VB)
        p = jnp.exp(mm(vec[at, :], q, NT) - lanes(freq[at, :]) - norm)
        if b == 0:
            p = jnp.concatenate([jnp.where(is_pair(pos_ref), 0.0, p[:PAIRS]), p[PAIRS:]], axis=0)
        weight[at, :] = p.astype(bf16)
    o_ref[...] = mm(turned[...], weight[...]).T.astype(bf16)


def vec_kernel(pos_ref, vec, freq, parts_ref, q_ref, unread_ref, same_ref, other_ref, lse, coef):
    @pl.when(pl.program_id(0) == 0)
    def _():
        top = parts_ref[0]
        for a in range(1, NA):
            top = jnp.maximum(top, parts_ref[a])
        total = jnp.exp(parts_ref[0] - top)
        for a in range(1, NA):
            total = total + jnp.exp(parts_ref[a] - top)
        lse[...] = top + jnp.log(total)
        same_ref[...] = jnp.zeros_like(same_ref)
        other_ref[...] = jnp.zeros_like(other_ref)

    q = q_ref[...]
    scaled = q * jnp.asarray(score_scale, bf16)
    norm = query_lanes(lse)
    for b in range(0, VS, VB):
        at = slice(b, b + VB)
        p = jnp.exp(mm(vec[at, :], scaled, NT) - lanes(freq[at, :]) - norm)
        if b == 0:
            p = jnp.concatenate([jnp.where(is_pair(pos_ref), p[:PAIRS] - 1.0, p[:PAIRS]), p[PAIRS:]], axis=0)
        coef[at, :] = p.astype(bf16)
    for b in range(0, NB, 2):
        g = mm(coef[b * PAIRS : (b + 2) * PAIRS, :], q)
        ref = (same_ref, other_ref)[b // 4]
        ref[b % 4] += g[:PAIRS]
        ref[b % 4 + 1] += g[PAIRS:]


def combine_kernel(got_ref, parts_ref, q_ref, pay_ref, out_ref):
    parts = parts_ref[...]
    top = jnp.max(parts, axis=0, keepdims=True)
    lse = top + jnp.log(jnp.sum(jnp.exp(parts - top), axis=0, keepdims=True))
    shares = jnp.exp(parts - lse)
    q = q_ref[...].astype(f32)
    vec = pay_ref[0:PAIRS, :].astype(f32)
    line = pay_ref[PAIRS : PAIRS + 16, :].astype(f32)[0:1, :]
    own = jnp.sum(q * vec, axis=1, keepdims=True) * score_scale - column(line, PAIRS) - column(lse, PAIRS)
    total = (jnp.exp(own) - 1.0).astype(bf16).astype(f32) * vec
    for a in range(NA):
        total = total + got_ref[a].astype(f32) * column(shares[a : a + 1], PAIRS)
    out_ref[...] = total * score_scale


def back_kernel(*refs):
    parts, (emb_ref, hid_ref, w_out_ref, place_ref, ids_ref), out_ref = refs[:4], refs[4:9], refs[-1]
    total = parts[0][...]
    for part in parts[1:]:
        total = total + part[...]
    grad = (total * score_scale).astype(bf16)
    hid = hid_ref[...]
    hg = jnp.where(hid.astype(f32) > 0.0, mm(grad, w_out_ref[...], NT), 0.0).astype(bf16)
    scatter = (iota((OWNERS * SLOT, PAIRS), 0) == place_ref[:, 0:PAIRS]).astype(f32).astype(bf16)
    slots = mm(scatter, grad).reshape(OWNERS, SLOT, E)
    ids = ids_ref[...].reshape(OWNERS, 1, E)
    slots = jnp.where(iota((OWNERS, SLOT, E), 1) == CAP, ids, slots).astype(bf16).reshape(16, 2, SLOT, E)
    w_out_part = mm(hid, grad, TN)
    w_in_part = mm(emb_ref[...], hg, TN)
    pieces = []
    for part in (w_out_part, w_in_part):
        n = part.shape[0] // 8
        tiles = [part[:, k : k + 128].reshape(n, 1, 8, 128) for k in range(0, part.shape[1], 128)]
        pieces.append(jnp.concatenate(tiles, axis=1).reshape(16, 4, SLOT, 128).astype(bf16))
    for z in range(4):
        out_ref[:, :, z, :, 0:E] = slots
        for c in range(2):
            out_ref[:, c, z, :, E : E + 128] = pieces[c][:, z]


TB = 512


def active_kernel(table_ref, w_in_ref, active_ref):
    hid = jnp.maximum(mm(table_ref[...].astype(bf16), w_in_ref[...]), 0.0).astype(bf16)
    active_ref[...] = (hid.astype(f32) > 0.0).astype(f32).astype(bf16)


def update_kernel(ids_ref, got_ref, table_ref, accum_ref, active_ref, w_in_ref, w_out_ref, table_out, accum_out):
    base = pl.program_id(0) * TB
    onehot = (ids_ref[...] == iota((TB, 128 * SLOT), 0) + base).astype(f32).astype(bf16)
    vals = got_ref[:, :, 0:E].reshape(128 * SLOT, E)
    vg = mm(onehot, vals)
    high = vg.astype(bf16)
    low = (vg - high.astype(f32)).astype(bf16)
    table = table_ref[...]
    back = mm(high, w_out_ref[...], NT) + mm(low, w_out_ref[...], NT)
    hg = jnp.where(active_ref[...].astype(f32) > 0.0, back, 0.0).astype(bf16)
    g = vg + mm(hg, w_in_ref[...], NT)
    acc = accum_ref[...] + g * g
    accum_out[...] = acc
    table_out[...] = table - learn_rate * g / jnp.sqrt(acc)


def a2a(x, axes):
    return lax.all_to_all(x, axes, split_axis=0, concat_axis=0, tiled=True)


def shift(x, axis, k):
    n = 2 if axis == "c" else 4
    return lax.ppermute(x, axis, [(i, (i + k) % n) for i in range(n)])


def whole(n):
    return [pl.BlockSpec(memory_space=VMEM)] * n


def unread(n):
    return [pl.BlockSpec(memory_space=pl.ANY)] * n


def after(x, *others):
    return lax.optimization_barrier((x, *others))[0]


def const(*shape):
    return pl.BlockSpec(shape, lambda *_: (0,) * len(shape))


def local(queries, item_owner, item_row, log_freq, table, accum, w_in, w_out):
    here_x = lax.axis_index("x").astype(i32)
    here_z = lax.axis_index("z").astype(i32)
    req, place, pick, ids = call(
        slots_kernel,
        (
            sds((OWNERS, 128), i32),
            sds((1, 256), i32),
            sds((PAIRS, OWNERS * CAP), bf16),
            sds((OWNERS, E), f32),
        ),
        in_specs=whole(2),
        out_specs=tuple(whole(4)),
        scratch_shapes=[pltpu.VMEM((8, 256), i32)],
    )(item_owner.reshape(1, PAIRS), item_row.reshape(1, PAIRS))
    asked = a2a(req.reshape(OWNERS, 1, 128), SHARD)
    slab = jnp.zeros((QB, E), bf16)
    for k in range(4):
        block = shift(queries, "x", 4 - k) if k else queries
        slab = lax.dynamic_update_slice(slab, block, ((here_x + k) % 4 * PAIRS, 0))
    slabs = [slab] + [shift(slab, "z", 4 - k) for k in range(1, 4)]
    all_q = jnp.zeros((QS, E), bf16)
    for k in range(4):
        all_q = lax.dynamic_update_slice(all_q, slabs[k], ((here_z + k) % 4 * QB, 0))
    wanted = jnp.maximum(asked[:, 0, :CAP].reshape(OWNERS * CAP), 0)
    picked = table.at[wanted].get(mode="promise_in_bounds").astype(bf16)
    got = a2a(picked.reshape(OWNERS, CAP, E), SHARD).reshape(OWNERS * CAP, E)
    freq_row = jnp.pad(log_freq.reshape(1, PAIRS), ((0, 15), (0, 256 - PAIRS)))
    emb, hid, pay = call(
        tower_kernel,
        (sds((PAIRS, E), bf16), sds((PAIRS, H), bf16), sds((PAIRS + 16, E), bf16)),
        in_specs=whole(5) + unread(1),
        out_specs=tuple(whole(3)),
    )(got, pick, w_in, w_out, freq_row, slab)
    vecs = [pay] + [shift(pay, "y", k) for k in range(1, 4)]
    vecs = vecs + [shift(v, "c", 1) for v in vecs]

    part_lse = call(
        score_kernel,
        sds((NA, QS // 128, 128), f32),
        cost=(2 * VS * QS * E, VS * QS * 2, VS * QS),
        limit=LIMIT,
        in_specs=whole(NB + 1),
        out_specs=whole(1)[0],
        scratch_shapes=[pltpu.VMEM((VS, E), bf16), pltpu.VMEM((VS, 128), f32)] + [pltpu.VMEM((VS, PB), f32)] * 2,
    )(*vecs, all_q)
    all_lse = a2a(part_lse, A)
    here = here_z * 4 + here_x
    o, vec_all, freq_all = call(
        query_kernel,
        (sds((QS, E), bf16), sds((VS, E), bf16), sds((VS, 128), f32)),
        cost=(4 * VS * QS * E, VS * QS, VS * QS),
        limit=LIMIT,
        grid_spec=pltpu.PrefetchScalarGridSpec(
            num_scalar_prefetch=1,
            grid=(QS // QB,),
            in_specs=[const(PAIRS + 16, E)] * NB
            + [const(NA, QS // 128, 128), pl.BlockSpec((QB, E), lambda i, pos: (i, 0))],
            out_specs=(pl.BlockSpec((QB, E), lambda i, pos: (i, 0)), const(VS, E), const(VS, 128)),
            scratch_shapes=[pltpu.VMEM((E, VS), bf16), pltpu.VMEM((VS, QB), bf16)],
        ),
    )(here.reshape(1), *vecs, part_lse, all_q)
    same, other = call(
        vec_kernel,
        (sds((4, PAIRS, E), f32), sds((4, PAIRS, E), f32)),
        cost=(4 * VS * QS * E, VS * QS, VS * QS),
        limit=LIMIT,
        grid_spec=pltpu.PrefetchScalarGridSpec(
            num_scalar_prefetch=1,
            grid=(QS // QB,),
            in_specs=[
                const(VS, E),
                const(VS, 128),
                const(NA, QS // 128, 128),
                pl.BlockSpec((QB, E), lambda i, pos: (i, 0)),
                unread(1)[0],
            ],
            out_specs=(const(4, PAIRS, E), const(4, PAIRS, E)),
            scratch_shapes=[pltpu.VMEM((QS // 128, 128), f32), pltpu.VMEM((VS, QB), bf16)],
        ),
    )(here.reshape(1), vec_all, freq_all, all_lse, all_q, o)
    o_got = a2a(o.reshape(NA, PAIRS, E), A)

    from_core = shift(other, "c", 1)
    sums = [same[k] + from_core[k] for k in range(4)]
    parts = [sums[0]] + [shift(sums[k], "y", 4 - k) for k in range(1, 4)]
    out = call(
        back_kernel,
        sds((16, 2, 4, SLOT, E + 128), bf16),
        limit=SMALL,
        in_specs=whole(9) + unread(1),
        out_specs=whole(1)[0],
    )(*parts, emb, hid, w_out, place, ids, o_got)
    back = a2a(out.reshape(128, SLOT, E + 128), ALL)

    own = lax.dynamic_slice(all_lse.reshape(NA, QS), (0, here * PAIRS), (NA, PAIRS))
    query_grad = call(
        combine_kernel,
        sds((PAIRS, E), f32),
        limit=SMALL,
        in_specs=whole(4),
        out_specs=whole(1)[0],
    )(o_got, jnp.pad(own, ((0, 0), (0, 256 - PAIRS))), queries, pay)

    active = call(
        active_kernel,
        sds((ROWS, H), bf16),
        cost=(2 * ROWS * E * H, ROWS * (E * 4 + H * 2), 0),
        limit=SMALL,
        grid=(ROWS // TB,),
        in_specs=[pl.BlockSpec((TB, E), lambda i: (i, 0)), const(E, H)],
        out_specs=pl.BlockSpec((TB, H), lambda i: (i, 0)),
    )(table, w_in)
    w_sum = jnp.sum(back[:, :, E:].astype(f32), axis=0)
    w_sum = after(jnp.broadcast_to(w_sum.astype(bf16)[None], (128, SLOT, 128)), query_grad, active)
    w_all = a2a(w_sum, ALL).reshape(16, 2, 4, SLOT, 128).astype(f32)
    hi = back[:, CAP, 0:CAP].astype(i32)
    lo = back[:, CAP, 128 : 128 + CAP].astype(i32)
    row_ids = jnp.where(hi < 0, -1, hi * 256 + lo)
    row_ids = jnp.pad(row_ids, ((0, 0), (0, SLOT - CAP)), constant_values=-1).reshape(1, 128 * SLOT)
    table_new, accum_new = call(
        update_kernel,
        (sds((ROWS, E), f32), sds((ROWS, E), f32)),
        cost=(4 * ROWS * 2048 * E, 4 * ROWS * E * 4, 0),
        limit=LIMIT,
        grid=(ROWS // TB,),
        in_specs=[
            const(1, 128 * SLOT),
            const(128, SLOT, E + 128),
            pl.BlockSpec((TB, E), lambda i: (i, 0)),
            pl.BlockSpec((TB, E), lambda i: (i, 0)),
            pl.BlockSpec((TB, H), lambda i: (i, 0)),
            const(E, H),
            const(H, E),
        ],
        out_specs=(
            pl.BlockSpec((TB, E), lambda i: (i, 0)),
            pl.BlockSpec((TB, E), lambda i: (i, 0)),
        ),
    )(row_ids, back, table, accum, active, w_in, w_out)

    def tiles(x, rows, cols):
        return x.reshape(rows // 8, cols // 128, 8, 128).transpose(0, 2, 1, 3).reshape(rows, cols)

    w_out_grad = tiles(w_all[:, 0], H, E)
    w_in_grad = tiles(w_all[:, 1], E, H)
    return query_grad, table_new, accum_new, w_in_grad, w_out_grad


def solution(mesh):
    fine = Mesh(mesh.devices.reshape(4, 4, 2, 4), ALL)
    return jax.shard_map(
        local,
        mesh=fine,
        in_specs=(
            P(ALL, None),
            P(ALL, None),
            P(ALL),
            P(ALL),
            P(SHARD, None),
            P(SHARD, None),
            P(),
            P(),
        ),
        out_specs=(P(ALL, None), P(SHARD, None), P(SHARD, None), P(), P()),
        check_vma=False,
    )
```

```python
import functools

import jax
import jax.numpy as jnp
from jax import lax
from jax.experimental import pallas as pl
from jax.experimental.pallas import tpu as pltpu
from jax.sharding import Mesh, PartitionSpec as P

E = 256
H = 512
PAIRS = 192
ROWS = 2048
CAP = 12
SLOT = 16
OWNERS = 32
NA = 16
NB = 8
QS = NA * PAIRS
LINES = QS // 128
SENT = LINES + 8
PACK = 40
VS = NB * PAIRS
LIMIT = 20 << 20
LARGE = 58 << 20
SMALL = 24 << 20
score_scale = 0.0625
learn_rate = 0.1

SHARD = ("x", "y", "c")
ALL = ("x", "y", "c", "z")
A = ("z", "x")

f32 = jnp.float32
bf16 = jnp.bfloat16
i32 = jnp.int32
VMEM = pltpu.MemorySpace.VMEM
NT = (((1,), (1,)), ((), ()))
TN = (((0,), (0,)), ((), ()))


def mm(a, b, dims=(((1,), (0,)), ((), ()))):
    return lax.dot_general(a, b, dims, preferred_element_type=f32)


def iota(shape, axis):
    return lax.broadcasted_iota(i32, shape, axis)


def call(kernel, out_shape, *, cost=(0, 0, 0), limit=None, **kw):
    return pl.pallas_call(
        kernel,
        out_shape=out_shape,
        compiler_params=pltpu.CompilerParams(vmem_limit_bytes=limit),
        cost_estimate=pl.CostEstimate(flops=cost[0], bytes_accessed=cost[1], transcendentals=cost[2]),
        **kw,
    )


def sds(shape, dtype):
    return jax.ShapeDtypeStruct(shape, dtype)


def column(lanes, rows):
    n = lanes.shape[1]
    eye = iota((rows, n), 0) == iota((rows, n), 1)
    return jnp.sum(jnp.where(eye, lanes, jnp.zeros((), lanes.dtype)), axis=1, keepdims=True)


def slots_kernel(owner_ref, row_ref, req_ref, place_ref, pick_ref, pair):
    pair[...] = jnp.full((8, 256), -1, i32)
    pair[0:1, 0:PAIRS] = owner_ref[...]
    pair[1:2, 0:PAIRS] = row_ref[...]
    owner = pair[0:1, :]
    row = pair[1:2, :]
    mine = owner == iota((OWNERS, 256), 0)
    onehot = mine.astype(f32).astype(bf16)
    earlier = (iota((256, 256), 0) < iota((256, 256), 1)).astype(f32).astype(bf16)
    before = mm(onehot, earlier)
    slot = jnp.sum(jnp.where(mine, before, 0.0), axis=0, keepdims=True).astype(i32)
    here = slot == iota((128, 256), 0)
    low = jnp.where(here, (row & 255).astype(f32), 0.0).astype(bf16)
    high = jnp.where(here, ((row >> 8) + 1).astype(f32), 0.0).astype(bf16)
    lo = mm(onehot, low, NT)
    hi = mm(onehot, high, NT) - 1.0
    req_ref[...] = jnp.where(hi < 0.0, -1, (hi * 256.0 + lo).astype(i32))
    place = jnp.where(owner < 0, -1, owner * SLOT + slot)
    place_ref[...] = place
    flat = jnp.where(owner < 0, -1, owner * CAP + slot).astype(f32)
    col = column(flat, PAIRS).astype(i32)
    pick_ref[...] = (col == iota((PAIRS, OWNERS * CAP), 1)).astype(f32).astype(bf16)


COST = 8 << 30


def pass_kernel(in_ref, unread_ref, out_ref):
    out_ref[...] = in_ref[...]


def slab_kernel(x_ref, *refs):
    blocks, out_ref = refs[:4], refs[-1]
    for k in range(4):
        at = (x_ref[0] + k) % 4 * PAIRS
        out_ref[pl.ds(pl.multiple_of(at, 16), PAIRS), :] = blocks[k][...]


def tower_kernel(got_ref, pick_ref, w_in_ref, w_out_ref, freq_ref, *refs):
    emb_ref, hid_ref, pay_ref = refs[-3:]
    emb = mm(pick_ref[...], got_ref[...]).astype(bf16)
    emb_ref[...] = emb
    hid = jnp.maximum(mm(emb, w_in_ref[...]), 0.0).astype(bf16)
    hid_ref[...] = hid
    vec = (emb.astype(f32) + mm(hid, w_out_ref[...])).astype(bf16)
    pay_ref[0:PAIRS, :] = vec
    pay_ref[PAIRS : PAIRS + 16, :] = freq_ref[...]


QB = 768
VB = 384


def load_vecs(vec_refs, vec, freq):
    for b in range(len(vec_refs)):
        at = slice(b * PAIRS, (b + 1) * PAIRS)
        line = vec_refs[b][PAIRS : PAIRS + 16, :].astype(f32)[0:1, :]
        freq[at, :] = jnp.broadcast_to(column(line, PAIRS), (PAIRS, 128))
        vec[at, :] = vec_refs[b][0:PAIRS, :]


def lanes(col, n=QB):
    return jnp.concatenate([col] * (n // 128), axis=1)


PB = 512


def score_kernel(*refs):
    vec_refs, (q_ref, ids_ref, lse_ref, vec, freq, *scores) = refs[:NB], refs[NB:]
    lse_ref[:, LINES:SENT, :] = jnp.broadcast_to(ids_ref[...][None], (NA, 8, 128))
    load_vecs(vec_refs, vec, freq)
    tops = []
    for j in range(QS // PB + 1):
        top, total = None, jnp.zeros((8, PB), f32)
        if j < QS // PB:
            q = q_ref[j * PB : (j + 1) * PB, :] * jnp.asarray(score_scale, bf16)
        for b in range(0, VS, VB):
            at = slice(b, b + VB)
            if j < QS // PB:
                s = mm(vec[at, :], q, NT) - lanes(freq[at, :], PB)
                scores[j % 2][at, :] = s
                t = jnp.max(s.reshape(VB // 8, 8, PB), axis=0)
                top = t if top is None else jnp.maximum(top, t)
            if j > 0:
                e = jnp.exp(scores[(j - 1) % 2][at, :] - tops[j - 1])
                total = total + jnp.sum(e.reshape(VB // 8, 8, PB), axis=0)
        if j < QS // PB:
            tops.append(jnp.max(top, axis=0, keepdims=True))
        if j > 0:
            part = tops[j - 1] + jnp.log(jnp.sum(total, axis=0, keepdims=True))
            n = PB // 128
            for k in range(n):
                row = part[:, k * 128 : (k + 1) * 128].reshape(1, 1, 128)
                at = (j - 1) * n + k
                lse_ref[:, at : at + 1, :] = jnp.broadcast_to(row, (NA, 1, 128))


def is_pair(pos_ref):
    first = pos_ref[0] * PAIRS - pl.program_id(0) * QB
    return iota((PAIRS, QB), 0) + first == iota((PAIRS, QB), 1)


def query_lanes(rows_ref, *index):
    n = QB // 128
    at = pl.program_id(0) * n
    return jnp.concatenate([rows_ref[(*index, pl.ds(at + i, 1), slice(None))] for i in range(n)], axis=1)


def query_kernel(pos_ref, vec, freq, part_ref, q_ref, o_ref, turned, weight):
    @pl.when(pl.program_id(0) == 0)
    def _():
        for k in range(0, VS, 256):
            turned[:, k : k + 256] = vec[k : k + 256, :].astype(f32).T.astype(bf16)

    q = q_ref[...] * jnp.asarray(score_scale, bf16)
    norm = query_lanes(part_ref, 0).reshape(1, QB)
    for b in range(0, VS, VB):
        at = slice(b, b + VB)
        p = jnp.exp(mm(vec[at, :], q, NT) - lanes(freq[at, :]) - norm)
        if b == 0:
            p = jnp.concatenate([jnp.where(is_pair(pos_ref), 0.0, p[:PAIRS]), p[PAIRS:]], axis=0)
        weight[at, :] = p.astype(bf16)
    o_ref[...] = mm(turned[...], weight[...]).T.astype(bf16)


def vec_kernel(first, n, pos_ref, vec, freq, parts_ref, q_ref, g_ref, lse, coef):
    @pl.when(pl.program_id(0) == 0)
    def _():
        top = parts_ref[0]
        for a in range(1, NA):
            top = jnp.maximum(top, parts_ref[a])
        total = jnp.exp(parts_ref[0] - top)
        for a in range(1, NA):
            total = total + jnp.exp(parts_ref[a] - top)
        lse[...] = top + jnp.log(total)
        g_ref[...] = jnp.zeros_like(g_ref)

    q = q_ref[...]
    scaled = q * jnp.asarray(score_scale, bf16)
    norm = query_lanes(lse)
    for b in range(0, n, 2):
        m = min(2, n - b) * PAIRS
        at = slice((first + b) * PAIRS, (first + b) * PAIRS + m)
        p = jnp.exp(mm(vec[at, :], scaled, NT) - lanes(freq[at, :]) - norm)
        if first == 0:
            p = jnp.where(is_pair(pos_ref), p - 1.0, p)
        coef[b * PAIRS : b * PAIRS + m, :] = p.astype(bf16)
    for b in range(0, n, 2):
        m = min(2, n - b)
        g = mm(coef[b * PAIRS : (b + m) * PAIRS, :], q)
        for k in range(m):
            g_ref[b + k] += g[k * PAIRS : (k + 1) * PAIRS]


def combine_kernel(got_ref, parts_ref, q_ref, pay_ref, out_ref):
    parts = parts_ref[...]
    top = jnp.max(parts, axis=0, keepdims=True)
    lse = top + jnp.log(jnp.sum(jnp.exp(parts - top), axis=0, keepdims=True))
    shares = jnp.exp(parts - lse)
    q = q_ref[...].astype(f32)
    vec = pay_ref[0:PAIRS, :].astype(f32)
    line = pay_ref[PAIRS : PAIRS + 16, :].astype(f32)[0:1, :]
    own = jnp.sum(q * vec, axis=1, keepdims=True) * score_scale - column(line, PAIRS) - column(lse, PAIRS)
    total = (jnp.exp(own) - 1.0).astype(bf16).astype(f32) * vec
    for a in range(NA):
        total = total + got_ref[a].astype(f32) * column(shares[a : a + 1], PAIRS)
    out_ref[...] = total * score_scale


def back_kernel(*refs):
    parts, (emb_ref, hid_ref, w_out_ref, place_ref), out_ref = refs[:4], refs[4:8], refs[-1]
    total = parts[0][...]
    for part in parts[1:]:
        total = total + part[...]
    grad = (total * score_scale).astype(bf16)
    hid = hid_ref[...]
    hg = jnp.where(hid.astype(f32) > 0.0, mm(grad, w_out_ref[...], NT), 0.0).astype(bf16)
    scatter = (iota((OWNERS * SLOT, PAIRS), 0) == place_ref[:, 0:PAIRS]).astype(f32).astype(bf16)
    slots = mm(scatter, grad).reshape(16, 2, SLOT, E)
    pieces = []
    for part in (mm(hid, grad, TN), mm(emb_ref[...], hg, TN)):
        n = part.shape[0] // 8
        tiles = [part[:, k : k + 128].reshape(n, 1, 8, 128) for k in range(0, part.shape[1], 128)]
        pieces.append(jnp.concatenate(tiles, axis=1).reshape(16, 4, 2, 8, 128))
    top = iota((16, 8, 128), 1) < 4
    for c in range(2):
        left, right = slots[:, c, :, 0:128], slots[:, c, :, 128:E]
        for z in range(4):
            w0, w1 = pieces[c][:, z, 0], pieces[c][:, z, 1]
            rolled = jnp.concatenate([w1[:, 4:8], w1[:, 0:4]], axis=1)
            rows = [
                left[:, 0:8],
                jnp.where(top, left[:, 8:16], w0),
                right[:, 0:8],
                jnp.where(top, right[:, 8:16], w1),
                jnp.where(top, w0, rolled),
            ]
            out_ref[:, c, z] = jnp.concatenate(rows, axis=1).astype(bf16)


TB = 512


def active_kernel(table_ref, w_in_ref, active_ref):
    hid = jnp.maximum(mm(table_ref[...].astype(bf16), w_in_ref[...]), 0.0).astype(bf16)
    active_ref[...] = (hid.astype(f32) > 0.0).astype(f32).astype(bf16)


def update_kernel(ids_ref, got_ref, table_ref, accum_ref, active_ref, w_in_ref, w_out_ref, table_out, accum_out):
    base = pl.program_id(0) * TB
    onehot = (ids_ref[...] == iota((TB, 128 * SLOT), 0) + base).astype(f32).astype(bf16)
    vals = jnp.concatenate([got_ref[:, 0:SLOT, :], got_ref[:, SLOT : 2 * SLOT, :]], axis=2).reshape(128 * SLOT, E)
    vg = mm(onehot, vals)
    high = vg.astype(bf16)
    low = (vg - high.astype(f32)).astype(bf16)
    table = table_ref[...]
    back = mm(high, w_out_ref[...], NT) + mm(low, w_out_ref[...], NT)
    hg = jnp.where(active_ref[...].astype(f32) > 0.0, back, 0.0).astype(bf16)
    g = vg + mm(hg, w_in_ref[...], NT)
    acc = accum_ref[...] + g * g
    accum_out[...] = acc
    table_out[...] = table - learn_rate * g / jnp.sqrt(acc)


def a2a(x, axes):
    return lax.all_to_all(x, axes, split_axis=0, concat_axis=0, tiled=True)


def shift(x, axis, k):
    n = 2 if axis == "c" else 4
    return lax.ppermute(x, axis, [(i, (i + k) % n) for i in range(n)])


def whole(n):
    return [pl.BlockSpec(memory_space=VMEM)] * n


def unread(n):
    return [pl.BlockSpec(memory_space=pl.ANY)] * n


def after(x, *others):
    return lax.optimization_barrier((x, *others))[0]


def const(*shape):
    return pl.BlockSpec(shape, lambda *_: (0,) * len(shape))


def local(queries, item_owner, item_row, log_freq, table, accum, w_in, w_out):
    here_x = lax.axis_index("x").astype(i32)
    here_z = lax.axis_index("z").astype(i32)
    req, place, pick = call(
        slots_kernel,
        (
            sds((OWNERS, 128), i32),
            sds((1, 256), i32),
            sds((PAIRS, OWNERS * CAP), bf16),
        ),
        in_specs=whole(2),
        out_specs=tuple(whole(3)),
        scratch_shapes=[pltpu.VMEM((8, 256), i32)],
    )(item_owner.reshape(1, PAIRS), item_row.reshape(1, PAIRS))
    asked = a2a(req.reshape(OWNERS, 1, 128), SHARD)
    early = call(
        pass_kernel,
        sds((PAIRS, E), bf16),
        cost=(COST, 1 << 20, 0),
        limit=SMALL,
        in_specs=whole(1) + unread(1),
        out_specs=whole(1)[0],
    )(queries, req)
    blocks = [queries] + [shift(early, "x", 4 - k) for k in range(1, 4)]
    ids = asked[:, 0, :SLOT].astype(f32).reshape(OWNERS * SLOT // 128, 128)
    ids = jnp.pad(ids, ((0, 8 - OWNERS * SLOT // 128), (0, 0)))
    wanted = jnp.maximum(asked[:, 0, :CAP].reshape(OWNERS * CAP), 0)
    picked = table.at[wanted].get(mode="promise_in_bounds").astype(bf16)
    slab = call(
        slab_kernel,
        sds((QB, E), bf16),
        cost=(COST, 1 << 20, 0),
        limit=SMALL,
        in_specs=[pl.BlockSpec(memory_space=pltpu.MemorySpace.SMEM)] + whole(4) + unread(1),
        out_specs=whole(1)[0],
    )(here_x.reshape(1), *blocks, picked)
    above, below = shift(slab, "z", 3), shift(slab, "z", 1)
    half = QB // 2
    far = [shift(above[:half], "z", 3), shift(below[half:], "z", 1)]
    all_q = jnp.zeros((QS, E), bf16)
    for k, block in ((0, slab), (1, above), (3, below), (2, jnp.concatenate(far, axis=0))):
        all_q = lax.dynamic_update_slice(all_q, block, ((here_z + k) % 4 * QB, 0))
    got = a2a(picked.reshape(OWNERS, CAP, E), SHARD).reshape(OWNERS * CAP, E)
    freq_row = jnp.pad(log_freq.reshape(1, PAIRS), ((0, 15), (0, 256 - PAIRS)))
    emb, hid, pay = call(
        tower_kernel,
        (sds((PAIRS, E), bf16), sds((PAIRS, H), bf16), sds((PAIRS + 16, E), bf16)),
        cost=(24 << 30, 1 << 20, 0),
        in_specs=whole(5),
        out_specs=tuple(whole(3)),
    )(got, pick, w_in, w_out, freq_row)
    vecs = [pay] + [shift(pay, "y", k) for k in range(1, 4)]
    vecs = vecs + [shift(v, "c", 1) for v in vecs]

    part_lse, vec_all, freq_all = call(
        score_kernel,
        (sds((NA, SENT, 128), f32), sds((VS, E), bf16), sds((VS, 128), f32)),
        cost=(2 * VS * QS * E, VS * QS * 2, VS * QS),
        limit=LIMIT,
        in_specs=whole(NB + 2),
        out_specs=tuple(whole(3)),
        scratch_shapes=[pltpu.VMEM((VS, PB), f32)] * 2,
    )(*vecs, all_q, ids)
    all_lse = a2a(part_lse, A)
    here = here_z * 4 + here_x
    o = call(
        query_kernel,
        sds((QS, E), bf16),
        cost=(4 * VS * QS * E, VS * QS, VS * QS),
        limit=LIMIT,
        grid_spec=pltpu.PrefetchScalarGridSpec(
            num_scalar_prefetch=1,
            grid=(QS // QB,),
            in_specs=[
                const(VS, E),
                const(VS, 128),
                const(NA, SENT, 128),
                pl.BlockSpec((QB, E), lambda i, pos: (i, 0)),
            ],
            out_specs=pl.BlockSpec((QB, E), lambda i, pos: (i, 0)),
            scratch_shapes=[
                pltpu.VMEM((E, VS), bf16),
                pltpu.VMEM((VS, QB), bf16),
            ],
        ),
    )(here.reshape(1), vec_all, freq_all, part_lse, all_q)

    def vec_grads(first, n, wait):
        first_lse, _ = lax.optimization_barrier((all_lse, wait))
        return call(
            functools.partial(vec_kernel, first, n),
            sds((n, PAIRS, E), f32),
            cost=(4 * n * PAIRS * QS * E, n * PAIRS * QS, n * PAIRS * QS),
            limit=LIMIT,
            grid_spec=pltpu.PrefetchScalarGridSpec(
                num_scalar_prefetch=1,
                grid=(QS // QB,),
                in_specs=[
                    const(VS, E),
                    const(VS, 128),
                    const(NA, SENT, 128),
                    pl.BlockSpec((QB, E), lambda i, pos: (i, 0)),
                ],
                out_specs=const(n, PAIRS, E),
                scratch_shapes=[
                    pltpu.VMEM((SENT, 128), f32),
                    pltpu.VMEM((n * PAIRS, QB), bf16),
                ],
            ),
        )(here.reshape(1), vec_all, freq_all, first_lse, all_q)

    o_got = a2a(o.reshape(NA, PAIRS, E), A)

    other = vec_grads(4, 4, o)
    same = vec_grads(1, 3, other)
    from_core = shift(other, "c", 1)
    sums = [same[k - 1] + from_core[k] for k in range(1, 4)]
    parts = [shift(sums[k - 1], "y", 4 - k) for k in range(1, 4)]
    mine = vec_grads(0, 1, sums[2])
    parts = [mine.reshape(PAIRS, E) + from_core[0]] + parts
    out = call(
        back_kernel,
        sds((16, 2, 4, PACK, 128), bf16),
        limit=LARGE,
        in_specs=whole(8) + unread(1),
        out_specs=whole(1)[0],
    )(*parts, emb, hid, w_out, place, o_got)
    back = a2a(out.reshape(128, PACK, 128), ALL)

    own = lax.dynamic_slice(all_lse[:, :LINES].reshape(NA, QS), (0, here * PAIRS), (NA, PAIRS))
    query_grad = call(
        combine_kernel,
        sds((PAIRS, E), f32),
        limit=SMALL,
        in_specs=whole(4),
        out_specs=whole(1)[0],
    )(o_got, jnp.pad(own, ((0, 0), (0, 256 - PAIRS))), queries, pay)

    active = call(
        active_kernel,
        sds((ROWS, H), bf16),
        cost=(2 * ROWS * E * H, ROWS * (E * 4 + H * 2), 0),
        limit=SMALL,
        grid=(ROWS // TB,),
        in_specs=[pl.BlockSpec((TB, E), lambda i: (i, 0)), const(E, H)],
        out_specs=pl.BlockSpec((TB, H), lambda i: (i, 0)),
    )(table, w_in)
    w_sum = jnp.sum(back.astype(f32), axis=0)
    w_sum = jnp.concatenate([w_sum[32:36], w_sum[12:16], w_sum[36:40], w_sum[28:32]], axis=0)
    w_sum = after(jnp.broadcast_to(w_sum.astype(bf16)[None], (128, SLOT, 128)), query_grad, active)
    w_all = a2a(w_sum, ALL).reshape(16, 2, 4, SLOT, 128).astype(f32)
    row_ids = all_lse.reshape(4, 4, SENT, 128)[:, :, LINES : LINES + 4]
    row_ids = lax.dynamic_index_in_dim(row_ids, here_x, axis=1, keepdims=False)
    row_ids = row_ids.reshape(4, OWNERS, SLOT).transpose(1, 0, 2).reshape(1, 128 * SLOT).astype(i32)
    table_new, accum_new = call(
        update_kernel,
        (sds((ROWS, E), f32), sds((ROWS, E), f32)),
        cost=(4 * ROWS * 2048 * E, 4 * ROWS * E * 4, 0),
        limit=LARGE,
        grid=(ROWS // TB,),
        in_specs=[
            const(1, 128 * SLOT),
            const(128, PACK, 128),
            pl.BlockSpec((TB, E), lambda i: (i, 0)),
            pl.BlockSpec((TB, E), lambda i: (i, 0)),
            pl.BlockSpec((TB, H), lambda i: (i, 0)),
            const(E, H),
            const(H, E),
        ],
        out_specs=(
            pl.BlockSpec((TB, E), lambda i: (i, 0)),
            pl.BlockSpec((TB, E), lambda i: (i, 0)),
        ),
    )(row_ids, back, table, accum, active, w_in, w_out)

    def tiles(x, rows, cols):
        return x.reshape(rows // 8, cols // 128, 8, 128).transpose(0, 2, 1, 3).reshape(rows, cols)

    w_out_grad = tiles(w_all[:, 0], H, E)
    w_in_grad = tiles(w_all[:, 1], E, H)
    return query_grad, table_new, accum_new, w_in_grad, w_out_grad


def solution(mesh):
    fine = Mesh(mesh.devices.reshape(4, 4, 2, 4), ALL)
    return jax.shard_map(
        local,
        mesh=fine,
        in_specs=(
            P(ALL, None),
            P(ALL, None),
            P(ALL),
            P(ALL),
            P(SHARD, None),
            P(SHARD, None),
            P(),
            P(),
        ),
        out_specs=(P(ALL, None), P(SHARD, None), P(SHARD, None), P(), P()),
        check_vma=False,
    )
```

```python
import functools

import jax
import jax.numpy as jnp
from jax import lax
from jax.experimental import pallas as pl
from jax.experimental.pallas import tpu as pltpu
from jax.sharding import Mesh, PartitionSpec as P

E = 256
H = 512
PAIRS = 192
ROWS = 2048
CAP = 12
SLOT = 16
OWNERS = 32
NA = 16
NB = 8
QS = NA * PAIRS
LINES = QS // 128
SENT = LINES + 8
PACK = 40
VS = NB * PAIRS
LIMIT = 20 << 20
LARGE = 58 << 20
SMALL = 24 << 20
score_scale = 0.0625
learn_rate = 0.1

SHARD = ("x", "y", "c")
ALL = ("x", "y", "c", "z")
A = ("z", "x")

f32 = jnp.float32
bf16 = jnp.bfloat16
i32 = jnp.int32
VMEM = pltpu.MemorySpace.VMEM
HBM = pltpu.MemorySpace.HBM
NT = (((1,), (1,)), ((), ()))
TN = (((0,), (0,)), ((), ()))


def mm(a, b, dims=(((1,), (0,)), ((), ()))):
    return lax.dot_general(a, b, dims, preferred_element_type=f32)


def iota(shape, axis):
    return lax.broadcasted_iota(i32, shape, axis)


def call(kernel, out_shape, *, cost=(0, 0, 0), limit=None, **kw):
    return pl.pallas_call(
        kernel,
        out_shape=out_shape,
        compiler_params=pltpu.CompilerParams(vmem_limit_bytes=limit),
        cost_estimate=pl.CostEstimate(flops=cost[0], bytes_accessed=cost[1], transcendentals=cost[2]),
        **kw,
    )


def sds(shape, dtype):
    return jax.ShapeDtypeStruct(shape, dtype)


def column(lanes, rows):
    n = lanes.shape[1]
    eye = iota((rows, n), 0) == iota((rows, n), 1)
    return jnp.sum(jnp.where(eye, lanes, jnp.zeros((), lanes.dtype)), axis=1, keepdims=True)


def slots_kernel(owner_ref, row_ref, req_ref, place_ref, pick_ref, pair):
    pair[...] = jnp.full((8, 256), -1, i32)
    pair[0:1, 0:PAIRS] = owner_ref[...]
    pair[1:2, 0:PAIRS] = row_ref[...]
    owner = pair[0:1, :]
    row = pair[1:2, :]
    mine = owner == iota((OWNERS, 256), 0)
    onehot = mine.astype(f32).astype(bf16)
    earlier = (iota((256, 256), 0) < iota((256, 256), 1)).astype(f32).astype(bf16)
    before = mm(onehot, earlier)
    slot = jnp.sum(jnp.where(mine, before, 0.0), axis=0, keepdims=True).astype(i32)
    here = slot == iota((128, 256), 0)
    low = jnp.where(here, (row & 255).astype(f32), 0.0).astype(bf16)
    high = jnp.where(here, ((row >> 8) + 1).astype(f32), 0.0).astype(bf16)
    lo = mm(onehot, low, NT)
    hi = mm(onehot, high, NT) - 1.0
    req_ref[...] = jnp.where(hi < 0.0, -1, (hi * 256.0 + lo).astype(i32))
    place = jnp.where(owner < 0, -1, owner * SLOT + slot)
    place_ref[...] = place
    flat = jnp.where(owner < 0, -1, owner * CAP + slot).astype(f32)
    col = column(flat, PAIRS).astype(i32)
    pick_ref[...] = (col == iota((PAIRS, OWNERS * CAP), 1)).astype(f32).astype(bf16)


COST = 8 << 30


def pass_kernel(in_ref, unread_ref, out_ref):
    out_ref[...] = in_ref[...]


def slab_kernel(x_ref, *refs):
    blocks, out_ref = refs[:4], refs[-1]
    for k in range(4):
        at = (x_ref[0] + k) % 4 * PAIRS
        out_ref[pl.ds(pl.multiple_of(at, 16), PAIRS), :] = blocks[k][...]


def tower_kernel(got_ref, pick_ref, w_in_ref, w_out_ref, freq_ref, *refs):
    emb_ref, hid_ref, pay_ref = refs[-3:]
    emb = mm(pick_ref[...], got_ref[...]).astype(bf16)
    emb_ref[...] = emb
    hid = jnp.maximum(mm(emb, w_in_ref[...]), 0.0).astype(bf16)
    hid_ref[...] = hid
    vec = (emb.astype(f32) + mm(hid, w_out_ref[...])).astype(bf16)
    pay_ref[0:PAIRS, :] = vec
    pay_ref[PAIRS : PAIRS + 16, :] = freq_ref[...]


QB = 768
VB = 384


def load_vecs(vec_refs, vec, freq):
    for b in range(len(vec_refs)):
        at = slice(b * PAIRS, (b + 1) * PAIRS)
        line = vec_refs[b][PAIRS : PAIRS + 16, :].astype(f32)[0:1, :]
        freq[at, :] = jnp.broadcast_to(column(line, PAIRS), (PAIRS, 128))
        vec[at, :] = vec_refs[b][0:PAIRS, :]


def lanes(col, n=QB):
    return jnp.concatenate([col] * (n // 128), axis=1)


PB = 512


def score_kernel(*refs):
    vec_refs, (q_ref, ids_ref, lse_ref, part_ref, vec, freq, *scores) = refs[:NB], refs[NB:]
    lse_ref[:, LINES:SENT, :] = jnp.broadcast_to(ids_ref[...][None], (NA, 8, 128))
    load_vecs(vec_refs, vec, freq)
    tops = []
    for j in range(QS // PB + 1):
        top, total = None, jnp.zeros((8, PB), f32)
        if j < QS // PB:
            q = q_ref[j * PB : (j + 1) * PB, :] * jnp.asarray(score_scale, bf16)
        for b in range(0, VS, VB):
            at = slice(b, b + VB)
            if j < QS // PB:
                s = mm(vec[at, :], q, NT) - lanes(freq[at, :], PB)
                scores[j % 2][at, :] = s
                t = jnp.max(s.reshape(VB // 8, 8, PB), axis=0)
                top = t if top is None else jnp.maximum(top, t)
            if j > 0:
                e = jnp.exp(scores[(j - 1) % 2][at, :] - tops[j - 1])
                total = total + jnp.sum(e.reshape(VB // 8, 8, PB), axis=0)
        if j < QS // PB:
            tops.append(jnp.max(top, axis=0, keepdims=True))
        if j > 0:
            part = tops[j - 1] + jnp.log(jnp.sum(total, axis=0, keepdims=True))
            n = PB // 128
            for k in range(n):
                row = part[:, k * 128 : (k + 1) * 128].reshape(1, 1, 128)
                at = (j - 1) * n + k
                lse_ref[:, at : at + 1, :] = jnp.broadcast_to(row, (NA, 1, 128))
                part_ref[at : at + 1, :] = row.reshape(1, 128)


def is_pair(pos_ref):
    first = pos_ref[0] * PAIRS - pl.program_id(0) * QB
    return iota((PAIRS, QB), 0) + first == iota((PAIRS, QB), 1)


def query_lanes(rows_ref, *index):
    n = QB // 128
    at = pl.program_id(0) * n
    return jnp.concatenate([rows_ref[(*index, pl.ds(at + i, 1), slice(None))] for i in range(n)], axis=1)


def query_kernel(pos_ref, vec, freq, part_ref, q_ref, o_ref, turned, weight):
    @pl.when(pl.program_id(0) == 0)
    def _():
        for k in range(0, VS, 256):
            turned[:, k : k + 256] = vec[k : k + 256, :].astype(f32).T.astype(bf16)

    q = q_ref[...] * jnp.asarray(score_scale, bf16)
    norm = query_lanes(part_ref)
    for b in range(0, VS, VB):
        at = slice(b, b + VB)
        p = jnp.exp(mm(vec[at, :], q, NT) - lanes(freq[at, :]) - norm)
        if b == 0:
            p = jnp.concatenate([jnp.where(is_pair(pos_ref), 0.0, p[:PAIRS]), p[PAIRS:]], axis=0)
        weight[at, :] = p.astype(bf16)
    o_ref[...] = mm(turned[...], weight[...]).T.astype(bf16)


def vec_kernel(first, n, pos_ref, vec, freq, parts_ref, q_ref, g_ref, lse, coef):
    @pl.when(pl.program_id(0) == 0)
    def _():
        top = parts_ref[0]
        for a in range(1, NA):
            top = jnp.maximum(top, parts_ref[a])
        total = jnp.exp(parts_ref[0] - top)
        for a in range(1, NA):
            total = total + jnp.exp(parts_ref[a] - top)
        lse[...] = top + jnp.log(total)
        g_ref[...] = jnp.zeros_like(g_ref)

    q = q_ref[...]
    scaled = q * jnp.asarray(score_scale, bf16)
    norm = query_lanes(lse)
    for b in range(0, n, 2):
        m = min(2, n - b) * PAIRS
        at = slice((first + b) * PAIRS, (first + b) * PAIRS + m)
        p = jnp.exp(mm(vec[at, :], scaled, NT) - lanes(freq[at, :]) - norm)
        if first == 0:
            p = jnp.where(is_pair(pos_ref), p - 1.0, p)
        coef[b * PAIRS : b * PAIRS + m, :] = p.astype(bf16)
    for b in range(0, n, 2):
        m = min(2, n - b)
        g = mm(coef[b * PAIRS : (b + m) * PAIRS, :], q)
        for k in range(m):
            g_ref[b + k] += g[k * PAIRS : (k + 1) * PAIRS]


def combine_kernel(got_ref, parts_ref, q_ref, pay_ref, out_ref):
    parts = parts_ref[...]
    top = jnp.max(parts, axis=0, keepdims=True)
    lse = top + jnp.log(jnp.sum(jnp.exp(parts - top), axis=0, keepdims=True))
    shares = jnp.exp(parts - lse)
    q = q_ref[...].astype(f32)
    vec = pay_ref[0:PAIRS, :].astype(f32)
    line = pay_ref[PAIRS : PAIRS + 16, :].astype(f32)[0:1, :]
    own = jnp.sum(q * vec, axis=1, keepdims=True) * score_scale - column(line, PAIRS) - column(lse, PAIRS)
    total = (jnp.exp(own) - 1.0).astype(bf16).astype(f32) * vec
    for a in range(NA):
        total = total + got_ref[a].astype(f32) * column(shares[a : a + 1], PAIRS)
    out_ref[...] = total * score_scale


def back_kernel(*refs):
    parts, (emb_ref, hid_ref, w_out_ref, place_ref), out_ref = refs[:4], refs[4:8], refs[-1]
    total = parts[0][...]
    for part in parts[1:]:
        total = total + part[...]
    grad = (total * score_scale).astype(bf16)
    hid = hid_ref[...]
    hg = jnp.where(hid.astype(f32) > 0.0, mm(grad, w_out_ref[...], NT), 0.0).astype(bf16)
    scatter = (iota((OWNERS * SLOT, PAIRS), 0) == place_ref[:, 0:PAIRS]).astype(f32).astype(bf16)
    slots = mm(scatter, grad).reshape(16, 2, SLOT, E)
    pieces = []
    for part in (mm(hid, grad, TN), mm(emb_ref[...], hg, TN)):
        n = part.shape[0] // 8
        tiles = [part[:, k : k + 128].reshape(n, 1, 8, 128) for k in range(0, part.shape[1], 128)]
        pieces.append(jnp.concatenate(tiles, axis=1).reshape(16, 4, 2, 8, 128))
    top = iota((16, 8, 128), 1) < 4
    for c in range(2):
        left, right = slots[:, c, :, 0:128], slots[:, c, :, 128:E]
        for z in range(4):
            w0, w1 = pieces[c][:, z, 0], pieces[c][:, z, 1]
            rolled = jnp.concatenate([w1[:, 4:8], w1[:, 0:4]], axis=1)
            rows = [
                left[:, 0:8],
                jnp.where(top, left[:, 8:16], w0),
                right[:, 0:8],
                jnp.where(top, right[:, 8:16], w1),
                jnp.where(top, w0, rolled),
            ]
            out_ref[:, c, z] = jnp.concatenate(rows, axis=1).astype(bf16)


def sum_kernel(got_ref, out_ref):
    total = jnp.sum(got_ref[...].astype(f32), axis=0)
    total = jnp.concatenate([total[32:36], total[12:16], total[36:40], total[28:32]], axis=0)
    out_ref[...] = jnp.broadcast_to(total.astype(bf16)[None], (128, SLOT, 128))


TB = 512


def active_kernel(table_ref, w_in_ref, active_ref):
    hid = jnp.maximum(mm(table_ref[...].astype(bf16), w_in_ref[...]), 0.0).astype(bf16)
    active_ref[...] = (hid.astype(f32) > 0.0).astype(f32).astype(bf16)


def update_kernel(ids_ref, got_ref, table_ref, accum_ref, active_ref, w_in_ref, w_out_ref, table_out, accum_out):
    base = pl.program_id(0) * TB
    onehot = (ids_ref[...] == iota((TB, 128 * SLOT), 0) + base).astype(f32).astype(bf16)
    vals = jnp.concatenate([got_ref[:, 0:SLOT, :], got_ref[:, SLOT : 2 * SLOT, :]], axis=2).reshape(128 * SLOT, E)
    vg = mm(onehot, vals)
    high = vg.astype(bf16)
    low = (vg - high.astype(f32)).astype(bf16)
    table = table_ref[...]
    back = mm(high, w_out_ref[...], NT) + mm(low, w_out_ref[...], NT)
    hg = jnp.where(active_ref[...].astype(f32) > 0.0, back, 0.0).astype(bf16)
    g = vg + mm(hg, w_in_ref[...], NT)
    acc = accum_ref[...] + g * g
    accum_out[...] = acc
    table_out[...] = table - learn_rate * g / jnp.sqrt(acc)


def a2a(x, axes):
    return lax.all_to_all(x, axes, split_axis=0, concat_axis=0, tiled=True)


def shift(x, axis, k):
    n = 2 if axis == "c" else 4
    return lax.ppermute(x, axis, [(i, (i + k) % n) for i in range(n)])


def whole(n):
    return [pl.BlockSpec(memory_space=VMEM)] * n


def unread(n):
    return [pl.BlockSpec(memory_space=pl.ANY)] * n


def const(*shape):
    return pl.BlockSpec(shape, lambda *_: (0,) * len(shape))


def local(queries, item_owner, item_row, log_freq, table, accum, w_in, w_out):
    here_x = lax.axis_index("x").astype(i32)
    here_z = lax.axis_index("z").astype(i32)
    req, place, pick = call(
        slots_kernel,
        (
            sds((OWNERS, 128), i32),
            sds((1, 256), i32),
            sds((PAIRS, OWNERS * CAP), bf16),
        ),
        in_specs=whole(2),
        out_specs=tuple(whole(3)),
        scratch_shapes=[pltpu.VMEM((8, 256), i32)],
    )(item_owner.reshape(1, PAIRS), item_row.reshape(1, PAIRS))
    asked = a2a(req.reshape(OWNERS, 1, 128), SHARD)
    early = call(
        pass_kernel,
        sds((PAIRS, E), bf16),
        cost=(COST, 1 << 20, 0),
        limit=SMALL,
        in_specs=whole(1) + unread(1),
        out_specs=whole(1)[0],
    )(queries, req)
    blocks = [queries] + [shift(early, "x", 4 - k) for k in range(1, 4)]
    ids = asked[:, 0, :SLOT].astype(f32).reshape(OWNERS * SLOT // 128, 128)
    ids = jnp.pad(ids, ((0, 8 - OWNERS * SLOT // 128), (0, 0)))
    wanted = jnp.maximum(asked[:, 0, :CAP].reshape(OWNERS * CAP), 0)
    picked = table.at[wanted].get(mode="promise_in_bounds").astype(bf16)
    slab = call(
        slab_kernel,
        sds((QB, E), bf16),
        cost=(COST, 1 << 20, 0),
        limit=SMALL,
        in_specs=[pl.BlockSpec(memory_space=pltpu.MemorySpace.SMEM)] + whole(4) + unread(1),
        out_specs=whole(1)[0],
    )(here_x.reshape(1), *blocks, picked)
    above, below = shift(slab, "z", 3), shift(slab, "z", 1)
    half = QB // 2
    far = [shift(above[:half], "z", 3), shift(below[half:], "z", 1)]
    all_q = jnp.zeros((QS, E), bf16)
    for k, block in ((0, slab), (1, above), (3, below), (2, jnp.concatenate(far, axis=0))):
        all_q = lax.dynamic_update_slice(all_q, block, ((here_z + k) % 4 * QB, 0))
    got = a2a(picked.reshape(OWNERS, CAP, E), SHARD).reshape(OWNERS * CAP, E)
    freq_row = jnp.pad(log_freq.reshape(1, PAIRS), ((0, 15), (0, 256 - PAIRS)))
    emb, hid, pay = call(
        tower_kernel,
        (sds((PAIRS, E), bf16), sds((PAIRS, H), bf16), sds((PAIRS + 16, E), bf16)),
        cost=(24 << 30, 1 << 20, 0),
        in_specs=whole(5),
        out_specs=tuple(whole(3)),
    )(got, pick, w_in, w_out, freq_row)
    vecs = [pay] + [shift(pay, "y", k) for k in range(1, 4)]
    vecs = vecs + [shift(v, "c", 1) for v in vecs]

    sent_lse, part_lse, vec_all, freq_all = call(
        score_kernel,
        (HBM((NA, SENT, 128), f32), sds((LINES, 128), f32), sds((VS, E), bf16), sds((VS, 128), f32)),
        cost=(2 * VS * QS * E, VS * QS * 2, VS * QS),
        limit=LIMIT,
        in_specs=whole(NB + 2),
        out_specs=tuple(whole(4)),
        scratch_shapes=[pltpu.VMEM((VS, PB), f32)] * 2,
    )(*vecs, all_q, ids)
    all_lse = a2a(sent_lse, A)
    here = here_z * 4 + here_x
    o = call(
        query_kernel,
        HBM((QS, E), bf16),
        cost=(4 * VS * QS * E, VS * QS, VS * QS),
        limit=LIMIT,
        grid_spec=pltpu.PrefetchScalarGridSpec(
            num_scalar_prefetch=1,
            grid=(QS // QB,),
            in_specs=[
                const(VS, E),
                const(VS, 128),
                const(LINES, 128),
                pl.BlockSpec((QB, E), lambda i, pos: (i, 0)),
            ],
            out_specs=pl.BlockSpec((QB, E), lambda i, pos: (i, 0)),
            scratch_shapes=[
                pltpu.VMEM((E, VS), bf16),
                pltpu.VMEM((VS, QB), bf16),
            ],
        ),
    )(here.reshape(1), vec_all, freq_all, part_lse, all_q)

    def vec_grads(first, n, wait):
        first_lse, _ = lax.optimization_barrier((all_lse, wait))
        return call(
            functools.partial(vec_kernel, first, n),
            sds((n, PAIRS, E), f32),
            cost=(4 * n * PAIRS * QS * E, n * PAIRS * QS, n * PAIRS * QS),
            limit=LIMIT,
            grid_spec=pltpu.PrefetchScalarGridSpec(
                num_scalar_prefetch=1,
                grid=(QS // QB,),
                in_specs=[
                    const(VS, E),
                    const(VS, 128),
                    const(NA, SENT, 128),
                    pl.BlockSpec((QB, E), lambda i, pos: (i, 0)),
                ],
                out_specs=const(n, PAIRS, E),
                scratch_shapes=[
                    pltpu.VMEM((SENT, 128), f32),
                    pltpu.VMEM((n * PAIRS, QB), bf16),
                ],
            ),
        )(here.reshape(1), vec_all, freq_all, first_lse, all_q)

    o_got = a2a(o.reshape(NA, PAIRS, E), A)

    other = vec_grads(4, 4, o)
    same = vec_grads(1, 3, other)
    from_core = shift(other, "c", 1)
    sums = [same[k - 1] + from_core[k] for k in range(1, 4)]
    parts = [shift(sums[k - 1], "y", 4 - k) for k in range(1, 4)]
    mine = vec_grads(0, 1, sums[2])
    parts = [mine.reshape(PAIRS, E) + from_core[0]] + parts
    out = call(
        back_kernel,
        sds((16, 2, 4, PACK, 128), bf16),
        limit=LARGE,
        in_specs=whole(8) + unread(1),
        out_specs=whole(1)[0],
    )(*parts, emb, hid, w_out, place, o_got)
    back = a2a(out.reshape(128, PACK, 128), ALL)

    own = lax.dynamic_slice(all_lse[:, :LINES].reshape(NA, QS), (0, here * PAIRS), (NA, PAIRS))
    query_grad = call(
        combine_kernel,
        sds((PAIRS, E), f32),
        limit=SMALL,
        in_specs=whole(4),
        out_specs=whole(1)[0],
    )(o_got, jnp.pad(own, ((0, 0), (0, 256 - PAIRS))), queries, pay)

    active = call(
        active_kernel,
        sds((ROWS, H), bf16),
        cost=(2 * ROWS * E * H, ROWS * (E * 4 + H * 2), 0),
        limit=SMALL,
        grid=(ROWS // TB,),
        in_specs=[pl.BlockSpec((TB, E), lambda i: (i, 0)), const(E, H)],
        out_specs=pl.BlockSpec((TB, H), lambda i: (i, 0)),
    )(table, w_in)
    back, query_grad, active = lax.optimization_barrier((back, query_grad, active))
    w_sum = call(
        sum_kernel,
        HBM((128, SLOT, 128), bf16),
        limit=LIMIT,
        in_specs=whole(1),
        out_specs=whole(1)[0],
    )(back)
    w_all = a2a(w_sum, ALL).reshape(16, 2, 4, SLOT, 128).astype(f32)
    row_ids = all_lse.reshape(4, 4, SENT, 128)[:, :, LINES : LINES + 4]
    row_ids = lax.dynamic_index_in_dim(row_ids, here_x, axis=1, keepdims=False)
    row_ids = row_ids.reshape(4, OWNERS, SLOT).transpose(1, 0, 2).reshape(1, 128 * SLOT).astype(i32)
    table_new, accum_new = call(
        update_kernel,
        (sds((ROWS, E), f32), sds((ROWS, E), f32)),
        cost=(4 * ROWS * 2048 * E, 4 * ROWS * E * 4, 0),
        limit=LARGE,
        grid=(ROWS // TB,),
        in_specs=[
            const(1, 128 * SLOT),
            const(128, PACK, 128),
            pl.BlockSpec((TB, E), lambda i: (i, 0)),
            pl.BlockSpec((TB, E), lambda i: (i, 0)),
            pl.BlockSpec((TB, H), lambda i: (i, 0)),
            const(E, H),
            const(H, E),
        ],
        out_specs=(
            pl.BlockSpec((TB, E), lambda i: (i, 0)),
            pl.BlockSpec((TB, E), lambda i: (i, 0)),
        ),
    )(row_ids, back, table, accum, active, w_in, w_out)

    def tiles(x, rows, cols):
        return x.reshape(rows // 8, cols // 128, 8, 128).transpose(0, 2, 1, 3).reshape(rows, cols)

    w_out_grad = tiles(w_all[:, 0], H, E)
    w_in_grad = tiles(w_all[:, 1], E, H)
    return query_grad, table_new, accum_new, w_in_grad, w_out_grad


def solution(mesh):
    fine = Mesh(mesh.devices.reshape(4, 4, 2, 4), ALL)
    return jax.shard_map(
        local,
        mesh=fine,
        in_specs=(
            P(ALL, None),
            P(ALL, None),
            P(ALL),
            P(ALL),
            P(SHARD, None),
            P(SHARD, None),
            P(),
            P(),
        ),
        out_specs=(P(ALL, None), P(SHARD, None), P(SHARD, None), P(), P()),
        check_vma=False,
    )
```

```python
import functools

import jax
import jax.numpy as jnp
from jax import lax
from jax.experimental import pallas as pl
from jax.experimental.pallas import tpu as pltpu
from jax.sharding import Mesh, PartitionSpec as P

E = 256
H = 512
PAIRS = 192
ROWS = 2048
SLOT = 16
OWNERS = 32
NA = 16
NB = 8
QS = NA * PAIRS
LINES = QS // 128
SENT = LINES + 8
PACK = 40
VS = NB * PAIRS
LIMIT = 20 << 20
LARGE = 58 << 20
SMALL = 24 << 20
score_scale = 0.0625
learn_rate = 0.1

SHARD = ("x", "y", "c")
ALL = ("x", "y", "c", "z")
A = ("z", "x")

f32 = jnp.float32
bf16 = jnp.bfloat16
i32 = jnp.int32
VMEM = pltpu.MemorySpace.VMEM
HBM = pltpu.MemorySpace.HBM
NT = (((1,), (1,)), ((), ()))
TN = (((0,), (0,)), ((), ()))


def mm(a, b, dims=(((1,), (0,)), ((), ()))):
    return lax.dot_general(a, b, dims, preferred_element_type=f32)


def iota(shape, axis):
    return lax.broadcasted_iota(i32, shape, axis)


def call(kernel, out_shape, *, cost=(0, 0, 0), limit=None, **kw):
    return pl.pallas_call(
        kernel,
        out_shape=out_shape,
        compiler_params=pltpu.CompilerParams(vmem_limit_bytes=limit),
        cost_estimate=pl.CostEstimate(flops=cost[0], bytes_accessed=cost[1], transcendentals=cost[2]),
        **kw,
    )


def sds(shape, dtype):
    return jax.ShapeDtypeStruct(shape, dtype)


def column(lanes, rows):
    n = lanes.shape[1]
    eye = iota((rows, n), 0) == iota((rows, n), 1)
    return jnp.sum(jnp.where(eye, lanes, jnp.zeros((), lanes.dtype)), axis=1, keepdims=True)


def slots_kernel(owner_ref, row_ref, req_ref, place_ref, pick_ref, pair):
    pair[...] = jnp.full((8, 256), -1, i32)
    pair[0:1, 0:PAIRS] = owner_ref[...]
    pair[1:2, 0:PAIRS] = row_ref[...]
    owner = pair[0:1, :]
    row = pair[1:2, :]
    mine = owner == iota((OWNERS, 256), 0)
    onehot = mine.astype(f32).astype(bf16)
    earlier = (iota((256, 256), 0) < iota((256, 256), 1)).astype(f32).astype(bf16)
    before = mm(onehot, earlier)
    slot = jnp.sum(jnp.where(mine, before, 0.0), axis=0, keepdims=True).astype(i32)
    here = slot == iota((128, 256), 0)
    low = jnp.where(here, (row & 255).astype(f32), 0.0).astype(bf16)
    high = jnp.where(here, ((row >> 8) + 1).astype(f32), 0.0).astype(bf16)
    lo = mm(onehot, low, NT)
    hi = mm(onehot, high, NT) - 1.0
    req_ref[...] = jnp.where(hi < 0.0, -1, (hi * 256.0 + lo).astype(i32))
    place = jnp.where(owner < 0, -1, owner * SLOT + slot)
    place_ref[...] = place
    col = column(place.astype(f32), PAIRS).astype(i32)
    pick_ref[...] = (col == iota((PAIRS, OWNERS * SLOT), 1)).astype(f32).astype(bf16)


COST = 8 << 30


def pass_kernel(in_ref, unread_ref, out_ref):
    out_ref[...] = in_ref[...]


def slab_kernel(x_ref, *refs):
    blocks, out_ref = refs[:4], refs[-1]
    for k in range(4):
        at = (x_ref[0] + k) % 4 * PAIRS
        out_ref[pl.ds(pl.multiple_of(at, 16), PAIRS), :] = blocks[k][...]


def tower_kernel(got_ref, pick_ref, w_in_ref, w_out_ref, freq_ref, *refs):
    emb_ref, hid_ref, pay_ref = refs[-3:]
    emb = mm(pick_ref[...], got_ref[...]).astype(bf16)
    emb_ref[...] = emb
    hid = jnp.maximum(mm(emb, w_in_ref[...]), 0.0).astype(bf16)
    hid_ref[...] = hid
    vec = (emb.astype(f32) + mm(hid, w_out_ref[...])).astype(bf16)
    pay_ref[0:PAIRS, :] = vec
    pay_ref[PAIRS : PAIRS + 16, :] = freq_ref[...]


QB = 768
VB = 384


def load_vecs(vec_refs, rows):
    for b in range(len(vec_refs)):
        at = slice(b * PAIRS, (b + 1) * PAIRS)
        line = vec_refs[b][PAIRS : PAIRS + 16, :].astype(f32)[0:1, :]
        rows[at, E : E + 128] = jnp.broadcast_to(column(line, PAIRS), (PAIRS, 128)).astype(bf16)
        rows[at, 0:E] = vec_refs[b][0:PAIRS, :]


def products(rows, at, q):
    return mm(rows[at, 0:E], q, NT) - lanes(rows[at, E : E + 128].astype(f32), q.shape[0])


def lanes(col, n=QB):
    return jnp.concatenate([col] * (n // 128), axis=1)


PB = 512


def score_kernel(*refs):
    vec_refs, (q_ref, ids_ref, lse_ref, part_ref, rows, *scores) = refs[:NB], refs[NB:]
    lse_ref[:, LINES:SENT, :] = jnp.broadcast_to(ids_ref[...][None], (NA, 8, 128))
    load_vecs(vec_refs, rows)
    tops = []
    for j in range(QS // PB + 1):
        top, total = None, jnp.zeros((8, PB), f32)
        if j < QS // PB:
            q = q_ref[j * PB : (j + 1) * PB, :] * jnp.asarray(score_scale, bf16)
        for b in range(0, VS, VB):
            at = slice(b, b + VB)
            if j < QS // PB:
                s = products(rows, at, q)
                scores[j % 2][at, :] = s
                t = jnp.max(s.reshape(VB // 8, 8, PB), axis=0)
                top = t if top is None else jnp.maximum(top, t)
            if j > 0:
                e = jnp.exp(scores[(j - 1) % 2][at, :] - tops[j - 1])
                total = total + jnp.sum(e.reshape(VB // 8, 8, PB), axis=0)
        if j < QS // PB:
            tops.append(jnp.max(top, axis=0, keepdims=True))
        if j > 0:
            part = tops[j - 1] + jnp.log(jnp.sum(total, axis=0, keepdims=True))
            n = PB // 128
            for k in range(n):
                row = part[:, k * 128 : (k + 1) * 128].reshape(1, 1, 128)
                at = (j - 1) * n + k
                lse_ref[:, at : at + 1, :] = jnp.broadcast_to(row, (NA, 1, 128))
                part_ref[at : at + 1, :] = row.reshape(1, 128)


def is_pair(pos_ref):
    first = pos_ref[0] * PAIRS - pl.program_id(0) * QB
    return iota((PAIRS, QB), 0) + first == iota((PAIRS, QB), 1)


def query_lanes(rows_ref, *index):
    n = QB // 128
    at = pl.program_id(0) * n
    return jnp.concatenate([rows_ref[(*index, pl.ds(at + i, 1), slice(None))] for i in range(n)], axis=1)


def query_kernel(pos_ref, rows, part_ref, q_ref, o_ref, turned, weight):
    @pl.when(pl.program_id(0) == 0)
    def _():
        for k in range(0, VS, 256):
            turned[:, k : k + 256] = rows[k : k + 256, 0:E].astype(f32).T.astype(bf16)

    q = q_ref[...] * jnp.asarray(score_scale, bf16)
    norm = query_lanes(part_ref)
    for b in range(0, VS, VB):
        at = slice(b, b + VB)
        p = jnp.exp(products(rows, at, q) - norm)
        if b == 0:
            p = jnp.concatenate([jnp.where(is_pair(pos_ref), 0.0, p[:PAIRS]), p[PAIRS:]], axis=0)
        weight[at, :] = p.astype(bf16)
    o_ref[...] = mm(turned[...], weight[...]).T.astype(bf16)


def vec_kernel(first, n, pos_ref, rows, parts_ref, q_ref, g_ref, lse, coef):
    @pl.when(pl.program_id(0) == 0)
    def _():
        top = parts_ref[0]
        for a in range(1, NA):
            top = jnp.maximum(top, parts_ref[a])
        total = jnp.exp(parts_ref[0] - top)
        for a in range(1, NA):
            total = total + jnp.exp(parts_ref[a] - top)
        lse[...] = top + jnp.log(total)
        g_ref[...] = jnp.zeros_like(g_ref)

    q = q_ref[...]
    scaled = q * jnp.asarray(score_scale, bf16)
    norm = query_lanes(lse)
    for b in range(0, n, 2):
        m = min(2, n - b) * PAIRS
        at = slice((first + b) * PAIRS, (first + b) * PAIRS + m)
        p = jnp.exp(products(rows, at, scaled) - norm)
        if first == 0:
            p = jnp.where(is_pair(pos_ref), p - 1.0, p)
        coef[b * PAIRS : b * PAIRS + m, :] = p.astype(bf16)
    for b in range(0, n, 2):
        m = min(2, n - b)
        g = mm(coef[b * PAIRS : (b + m) * PAIRS, :], q)
        for k in range(m):
            g_ref[b + k] += g[k * PAIRS : (k + 1) * PAIRS]


def combine_kernel(got_ref, parts_ref, q_ref, pay_ref, out_ref):
    parts = parts_ref[...]
    top = jnp.max(parts, axis=0, keepdims=True)
    lse = top + jnp.log(jnp.sum(jnp.exp(parts - top), axis=0, keepdims=True))
    shares = jnp.exp(parts - lse)
    q = q_ref[...].astype(f32)
    vec = pay_ref[0:PAIRS, :].astype(f32)
    line = pay_ref[PAIRS : PAIRS + 16, :].astype(f32)[0:1, :]
    own = jnp.sum(q * vec, axis=1, keepdims=True) * score_scale - column(line, PAIRS) - column(lse, PAIRS)
    total = (jnp.exp(own) - 1.0).astype(bf16).astype(f32) * vec
    for a in range(NA):
        total = total + got_ref[a].astype(f32) * column(shares[a : a + 1], PAIRS)
    out_ref[...] = total * score_scale


def back_kernel(*refs):
    parts, (emb_ref, hid_ref, w_out_ref, place_ref), out_ref = refs[:4], refs[4:8], refs[-1]
    total = parts[0][...]
    for part in parts[1:]:
        total = total + part[...]
    grad = (total * score_scale).astype(bf16)
    hid = hid_ref[...]
    hg = jnp.where(hid.astype(f32) > 0.0, mm(grad, w_out_ref[...], NT), 0.0).astype(bf16)
    scatter = (iota((OWNERS * SLOT, PAIRS), 0) == place_ref[:, 0:PAIRS]).astype(f32).astype(bf16)
    slots = mm(scatter, grad).reshape(16, 2, SLOT, E)
    pieces = []
    for part in (mm(hid, grad, TN), mm(emb_ref[...], hg, TN)):
        n = part.shape[0] // 8
        tiles = [part[:, k : k + 128].reshape(n, 1, 8, 128) for k in range(0, part.shape[1], 128)]
        pieces.append(jnp.concatenate(tiles, axis=1).reshape(16, 4, 2, 8, 128))
    top = iota((16, 8, 128), 1) < 4
    for c in range(2):
        left, right = slots[:, c, :, 0:128], slots[:, c, :, 128:E]
        for z in range(4):
            w0, w1 = pieces[c][:, z, 0], pieces[c][:, z, 1]
            rolled = jnp.concatenate([w1[:, 4:8], w1[:, 0:4]], axis=1)
            rows = [
                left[:, 0:8],
                jnp.where(top, left[:, 8:16], w0),
                right[:, 0:8],
                jnp.where(top, right[:, 8:16], w1),
                jnp.where(top, w0, rolled),
            ]
            out_ref[:, c, z] = jnp.concatenate(rows, axis=1).astype(bf16)


def sum_kernel(got_ref, out_ref):
    total = jnp.sum(got_ref[...].astype(f32), axis=0)
    total = jnp.concatenate([total[32:36], total[12:16], total[36:40], total[28:32]], axis=0)
    out_ref[...] = jnp.broadcast_to(total.astype(bf16)[None], (128, SLOT, 128))


TB = 512


def active_kernel(table_ref, w_in_ref, active_ref):
    hid = jnp.maximum(mm(table_ref[...].astype(bf16), w_in_ref[...]), 0.0).astype(bf16)
    active_ref[...] = (hid.astype(f32) > 0.0).astype(f32).astype(bf16)


def update_kernel(ids_ref, got_ref, table_ref, accum_ref, active_ref, w_in_ref, w_out_ref, table_out, accum_out):
    base = pl.program_id(0) * TB
    onehot = (ids_ref[...] == iota((TB, 128 * SLOT), 0) + base).astype(f32).astype(bf16)
    vals = jnp.concatenate([got_ref[:, 0:SLOT, :], got_ref[:, SLOT : 2 * SLOT, :]], axis=2).reshape(128 * SLOT, E)
    vg = mm(onehot, vals)
    high = vg.astype(bf16)
    low = (vg - high.astype(f32)).astype(bf16)
    table = table_ref[...]
    back = mm(high, w_out_ref[...], NT) + mm(low, w_out_ref[...], NT)
    hg = jnp.where(active_ref[...].astype(f32) > 0.0, back, 0.0).astype(bf16)
    g = vg + mm(hg, w_in_ref[...], NT)
    acc = accum_ref[...] + g * g
    accum_out[...] = acc
    table_out[...] = table - learn_rate * g / jnp.sqrt(acc)


def a2a(x, axes):
    return lax.all_to_all(x, axes, split_axis=0, concat_axis=0, tiled=True)


def shift(x, axis, k):
    n = 2 if axis == "c" else 4
    return lax.ppermute(x, axis, [(i, (i + k) % n) for i in range(n)])


def whole(n):
    return [pl.BlockSpec(memory_space=VMEM)] * n


def unread(n):
    return [pl.BlockSpec(memory_space=pl.ANY)] * n


def const(*shape):
    return pl.BlockSpec(shape, lambda *_: (0,) * len(shape))


def local(queries, item_owner, item_row, log_freq, table, accum, w_in, w_out):
    here_x = lax.axis_index("x").astype(i32)
    here_z = lax.axis_index("z").astype(i32)
    req, place, pick = call(
        slots_kernel,
        (
            sds((OWNERS, 128), i32),
            sds((1, 256), i32),
            sds((PAIRS, OWNERS * SLOT), bf16),
        ),
        in_specs=whole(2),
        out_specs=tuple(whole(3)),
        scratch_shapes=[pltpu.VMEM((8, 256), i32)],
    )(item_owner.reshape(1, PAIRS), item_row.reshape(1, PAIRS))
    asked = a2a(req.reshape(OWNERS, 1, 128), SHARD)
    early = call(
        pass_kernel,
        sds((PAIRS, E), bf16),
        cost=(COST, 1 << 20, 0),
        limit=SMALL,
        in_specs=whole(1) + unread(1),
        out_specs=whole(1)[0],
    )(queries, req)
    blocks = [queries] + [shift(early, "x", 4 - k) for k in range(1, 4)]
    ids = asked[:, 0, :SLOT].astype(f32).reshape(OWNERS * SLOT // 128, 128)
    ids = jnp.pad(ids, ((0, 8 - OWNERS * SLOT // 128), (0, 0)))
    wanted = jnp.maximum(asked[:, 0, :SLOT].reshape(OWNERS * SLOT), 0)
    picked = table.at[wanted].get(mode="promise_in_bounds").astype(bf16)
    slab = call(
        slab_kernel,
        sds((QB, E), bf16),
        cost=(COST, 1 << 20, 0),
        limit=SMALL,
        in_specs=[pl.BlockSpec(memory_space=pltpu.MemorySpace.SMEM)] + whole(4) + unread(1),
        out_specs=whole(1)[0],
    )(here_x.reshape(1), *blocks, picked)
    above, below = shift(slab, "z", 3), shift(slab, "z", 1)
    half = QB // 2
    far = [shift(above[:half], "z", 3), shift(below[half:], "z", 1)]
    all_q = jnp.zeros((QS, E), bf16)
    for k, block in ((0, slab), (1, above), (3, below), (2, jnp.concatenate(far, axis=0))):
        all_q = lax.dynamic_update_slice(all_q, block, ((here_z + k) % 4 * QB, 0))
    got = a2a(picked.reshape(OWNERS, SLOT, E), SHARD).reshape(OWNERS * SLOT, E)
    freq_row = jnp.pad(log_freq.reshape(1, PAIRS), ((0, 15), (0, 256 - PAIRS)))
    emb, hid, pay = call(
        tower_kernel,
        (sds((PAIRS, E), bf16), sds((PAIRS, H), bf16), sds((PAIRS + 16, E), bf16)),
        cost=(24 << 30, 1 << 20, 0),
        in_specs=whole(5),
        out_specs=tuple(whole(3)),
    )(got, pick, w_in, w_out, freq_row)
    vecs = [pay] + [shift(pay, "y", k) for k in range(1, 4)]
    vecs = vecs + [shift(v, "c", 1) for v in vecs]

    sent_lse, part_lse, vec_rows = call(
        score_kernel,
        (HBM((NA, SENT, 128), f32), sds((LINES, 128), f32), sds((VS, E + 128), bf16)),
        cost=(2 * VS * QS * E, VS * QS * 2, VS * QS),
        limit=LIMIT,
        in_specs=whole(NB + 2),
        out_specs=tuple(whole(3)),
        scratch_shapes=[pltpu.VMEM((VS, PB), f32)] * 2,
    )(*vecs, all_q, ids)
    all_lse = a2a(sent_lse, A)
    here = here_z * 4 + here_x
    o = call(
        query_kernel,
        HBM((QS, E), bf16),
        cost=(4 * VS * QS * E, VS * QS, VS * QS),
        limit=LIMIT,
        grid_spec=pltpu.PrefetchScalarGridSpec(
            num_scalar_prefetch=1,
            grid=(QS // QB,),
            in_specs=[
                const(VS, E + 128),
                const(LINES, 128),
                pl.BlockSpec((QB, E), lambda i, pos: (i, 0)),
            ],
            out_specs=pl.BlockSpec((QB, E), lambda i, pos: (i, 0)),
            scratch_shapes=[
                pltpu.VMEM((E, VS), bf16),
                pltpu.VMEM((VS, QB), bf16),
            ],
        ),
    )(here.reshape(1), vec_rows, part_lse, all_q)

    def vec_grads(first, n, wait):
        first_lse, _ = lax.optimization_barrier((all_lse, wait))
        return call(
            functools.partial(vec_kernel, first, n),
            sds((n, PAIRS, E), f32),
            cost=(4 * n * PAIRS * QS * E, n * PAIRS * QS, n * PAIRS * QS),
            limit=LIMIT,
            grid_spec=pltpu.PrefetchScalarGridSpec(
                num_scalar_prefetch=1,
                grid=(QS // QB,),
                in_specs=[
                    const(VS, E + 128),
                    const(NA, SENT, 128),
                    pl.BlockSpec((QB, E), lambda i, pos: (i, 0)),
                ],
                out_specs=const(n, PAIRS, E),
                scratch_shapes=[
                    pltpu.VMEM((SENT, 128), f32),
                    pltpu.VMEM((n * PAIRS, QB), bf16),
                ],
            ),
        )(here.reshape(1), vec_rows, first_lse, all_q)

    o_got = a2a(o.reshape(NA, PAIRS, E), A)

    other = vec_grads(4, 4, o)
    same = vec_grads(1, 3, other)
    from_core = shift(other, "c", 1)
    sums = [same[k - 1] + from_core[k] for k in range(1, 4)]
    parts = [shift(sums[k - 1], "y", 4 - k) for k in range(1, 4)]
    mine = vec_grads(0, 1, sums[2])
    parts = [mine.reshape(PAIRS, E) + from_core[0]] + parts
    out = call(
        back_kernel,
        sds((16, 2, 4, PACK, 128), bf16),
        limit=LARGE,
        in_specs=whole(8) + unread(1),
        out_specs=whole(1)[0],
    )(*parts, emb, hid, w_out, place, o_got)
    back = a2a(out.reshape(128, PACK, 128), ALL)

    own = lax.dynamic_slice(all_lse[:, :LINES].reshape(NA, QS), (0, here * PAIRS), (NA, PAIRS))
    query_grad = call(
        combine_kernel,
        sds((PAIRS, E), f32),
        limit=SMALL,
        in_specs=whole(4),
        out_specs=whole(1)[0],
    )(o_got, jnp.pad(own, ((0, 0), (0, 256 - PAIRS))), queries, pay)

    active = call(
        active_kernel,
        sds((ROWS, H), bf16),
        cost=(2 * ROWS * E * H, ROWS * (E * 4 + H * 2), 0),
        limit=SMALL,
        grid=(ROWS // TB,),
        in_specs=[pl.BlockSpec((TB, E), lambda i: (i, 0)), const(E, H)],
        out_specs=pl.BlockSpec((TB, H), lambda i: (i, 0)),
    )(table, w_in)
    back, query_grad, active = lax.optimization_barrier((back, query_grad, active))
    w_sum = call(
        sum_kernel,
        HBM((128, SLOT, 128), bf16),
        limit=LIMIT,
        in_specs=whole(1),
        out_specs=whole(1)[0],
    )(back)
    w_all = a2a(w_sum, ALL).reshape(16, 2, 4, SLOT, 128).astype(f32)
    row_ids = all_lse.reshape(4, 4, SENT, 128)[:, :, LINES : LINES + 4]
    row_ids = lax.dynamic_index_in_dim(row_ids, here_x, axis=1, keepdims=False)
    row_ids = row_ids.reshape(4, OWNERS, SLOT).transpose(1, 0, 2).reshape(1, 128 * SLOT).astype(i32)
    table_new, accum_new = call(
        update_kernel,
        (sds((ROWS, E), f32), sds((ROWS, E), f32)),
        cost=(4 * ROWS * 2048 * E, 4 * ROWS * E * 4, 0),
        limit=LARGE,
        grid=(ROWS // TB,),
        in_specs=[
            const(1, 128 * SLOT),
            const(128, PACK, 128),
            pl.BlockSpec((TB, E), lambda i: (i, 0)),
            pl.BlockSpec((TB, E), lambda i: (i, 0)),
            pl.BlockSpec((TB, H), lambda i: (i, 0)),
            const(E, H),
            const(H, E),
        ],
        out_specs=(
            pl.BlockSpec((TB, E), lambda i: (i, 0)),
            pl.BlockSpec((TB, E), lambda i: (i, 0)),
        ),
    )(row_ids, back, table, accum, active, w_in, w_out)

    def tiles(x, rows, cols):
        return x.reshape(rows // 8, cols // 128, 8, 128).transpose(0, 2, 1, 3).reshape(rows, cols)

    w_out_grad = tiles(w_all[:, 0], H, E)
    w_in_grad = tiles(w_all[:, 1], E, H)
    return query_grad, table_new, accum_new, w_in_grad, w_out_grad


def solution(mesh):
    fine = Mesh(mesh.devices.reshape(4, 4, 2, 4), ALL)
    return jax.shard_map(
        local,
        mesh=fine,
        in_specs=(
            P(ALL, None),
            P(ALL, None),
            P(ALL),
            P(ALL),
            P(SHARD, None),
            P(SHARD, None),
            P(),
            P(),
        ),
        out_specs=(P(ALL, None), P(SHARD, None), P(SHARD, None), P(), P()),
        check_vma=False,
    )
```

```python
import functools

import jax
import jax.numpy as jnp
from jax import lax
from jax.experimental import pallas as pl
from jax.experimental.pallas import tpu as pltpu
from jax.sharding import Mesh, PartitionSpec as P

E = 256
H = 512
PAIRS = 192
ROWS = 2048
SLOT = 16
OWNERS = 32
NA = 16
NB = 8
QS = NA * PAIRS
LINES = QS // 128
SENT = LINES + 8
PACK = 40
VS = NB * PAIRS
LIMIT = 20 << 20
LARGE = 58 << 20
SMALL = 24 << 20
score_scale = 0.0625
learn_rate = 0.1

SHARD = ("x", "y", "c")
ALL = ("x", "y", "c", "z")
A = ("z", "x")

f32 = jnp.float32
bf16 = jnp.bfloat16
i32 = jnp.int32
VMEM = pltpu.MemorySpace.VMEM
HBM = pltpu.MemorySpace.HBM
NT = (((1,), (1,)), ((), ()))
TN = (((0,), (0,)), ((), ()))


def mm(a, b, dims=(((1,), (0,)), ((), ()))):
    return lax.dot_general(a, b, dims, preferred_element_type=f32)


def iota(shape, axis):
    return lax.broadcasted_iota(i32, shape, axis)


def call(kernel, out_shape, *, cost=(0, 0, 0), limit=None, **kw):
    return pl.pallas_call(
        kernel,
        out_shape=out_shape,
        compiler_params=pltpu.CompilerParams(vmem_limit_bytes=limit),
        cost_estimate=pl.CostEstimate(flops=cost[0], bytes_accessed=cost[1], transcendentals=cost[2]),
        **kw,
    )


def sds(shape, dtype):
    return jax.ShapeDtypeStruct(shape, dtype)


def column(lanes, rows):
    n = lanes.shape[1]
    eye = iota((rows, n), 0) == iota((rows, n), 1)
    return jnp.sum(jnp.where(eye, lanes, jnp.zeros((), lanes.dtype)), axis=1, keepdims=True)


def slots_kernel(owner_ref, row_ref, req_ref, place_ref, pick_ref, pair):
    pair[...] = jnp.full((8, 256), -1, i32)
    pair[0:1, 0:PAIRS] = owner_ref[...]
    pair[1:2, 0:PAIRS] = row_ref[...]
    owner = pair[0:1, :]
    row = pair[1:2, :]
    mine = owner == iota((OWNERS, 256), 0)
    onehot = mine.astype(f32).astype(bf16)
    earlier = (iota((256, 256), 0) < iota((256, 256), 1)).astype(f32).astype(bf16)
    before = mm(onehot, earlier)
    slot = jnp.sum(jnp.where(mine, before, 0.0), axis=0, keepdims=True).astype(i32)
    here = slot == iota((128, 256), 0)
    low = jnp.where(here, (row & 255).astype(f32), 0.0).astype(bf16)
    high = jnp.where(here, ((row >> 8) + 1).astype(f32), 0.0).astype(bf16)
    lo = mm(onehot, low, NT)
    hi = mm(onehot, high, NT) - 1.0
    req_ref[...] = jnp.where(hi < 0.0, -1, (hi * 256.0 + lo).astype(i32))
    place = jnp.where(owner < 0, -1, owner * SLOT + slot)
    place_ref[...] = place
    col = column(place.astype(f32), PAIRS).astype(i32)
    pick_ref[...] = (col == iota((PAIRS, OWNERS * SLOT), 1)).astype(f32).astype(bf16)


COST = 8 << 30


def pass_kernel(in_ref, unread_ref, out_ref):
    out_ref[...] = in_ref[...]


def slab_kernel(x_ref, *refs):
    blocks, out_ref = refs[:4], refs[-1]
    for k in range(4):
        at = (x_ref[0] + k) % 4 * PAIRS
        out_ref[pl.ds(pl.multiple_of(at, 16), PAIRS), :] = blocks[k][...]


def tower_kernel(got_ref, pick_ref, w_in_ref, w_out_ref, freq_ref, *refs):
    emb_ref, hid_ref, pay_ref = refs[-3:]
    emb = mm(pick_ref[...], got_ref[...]).astype(bf16)
    emb_ref[...] = emb
    hid = jnp.maximum(mm(emb, w_in_ref[...]), 0.0).astype(bf16)
    hid_ref[...] = hid
    vec = (emb.astype(f32) + mm(hid, w_out_ref[...])).astype(bf16)
    pay_ref[0:PAIRS, :] = vec
    pay_ref[PAIRS : PAIRS + 16, :] = freq_ref[...]


QB = 768
VB = 384


def load_vecs(vec_refs, rows):
    for b in range(len(vec_refs)):
        at = slice(b * PAIRS, (b + 1) * PAIRS)
        line = vec_refs[b][PAIRS : PAIRS + 16, :].astype(f32)[0:1, :]
        rows[at, E : E + 128] = jnp.broadcast_to(column(line, PAIRS), (PAIRS, 128)).astype(bf16)
        rows[at, 0:E] = vec_refs[b][0:PAIRS, :]


def products(rows, at, q):
    return mm(rows[at, 0:E], q, NT) - lanes(rows[at, E : E + 128].astype(f32), q.shape[0])


def lanes(col, n=QB):
    return jnp.concatenate([col] * (n // 128), axis=1)


PB = 512


def score_kernel(*refs):
    vec_refs, (q_ref, ids_ref, lse_ref, part_ref, rows, *scores) = refs[:NB], refs[NB:]
    lse_ref[:, LINES:SENT, :] = jnp.broadcast_to(ids_ref[...][None], (NA, 8, 128))
    load_vecs(vec_refs, rows)
    tops = []
    for j in range(QS // PB + 1):
        top, total = None, jnp.zeros((8, PB), f32)
        if j < QS // PB:
            q = q_ref[j * PB : (j + 1) * PB, :] * jnp.asarray(score_scale, bf16)
        for b in range(0, VS, VB):
            at = slice(b, b + VB)
            if j < QS // PB:
                s = products(rows, at, q)
                scores[j % 2][at, :] = s
                t = jnp.max(s.reshape(VB // 8, 8, PB), axis=0)
                top = t if top is None else jnp.maximum(top, t)
            if j > 0:
                e = jnp.exp(scores[(j - 1) % 2][at, :] - tops[j - 1])
                total = total + jnp.sum(e.reshape(VB // 8, 8, PB), axis=0)
        if j < QS // PB:
            tops.append(jnp.max(top, axis=0, keepdims=True))
        if j > 0:
            part = tops[j - 1] + jnp.log(jnp.sum(total, axis=0, keepdims=True))
            n = PB // 128
            for k in range(n):
                row = part[:, k * 128 : (k + 1) * 128].reshape(1, 1, 128)
                at = (j - 1) * n + k
                lse_ref[:, at : at + 1, :] = jnp.broadcast_to(row, (NA, 1, 128))
                part_ref[at : at + 1, :] = row.reshape(1, 128)


def is_pair(pos_ref):
    first = pos_ref[0] * PAIRS - pl.program_id(0) * QB
    return iota((PAIRS, QB), 0) + first == iota((PAIRS, QB), 1)


def query_lanes(rows_ref, *index):
    n = QB // 128
    at = pl.program_id(0) * n
    return jnp.concatenate([rows_ref[(*index, pl.ds(at + i, 1), slice(None))] for i in range(n)], axis=1)


def query_kernel(pos_ref, rows, part_ref, q_ref, o_ref, turned, weight):
    @pl.when(pl.program_id(0) == 0)
    def _():
        for k in range(0, VS, 256):
            turned[:, k : k + 256] = rows[k : k + 256, 0:E].astype(f32).T.astype(bf16)

    q = q_ref[...] * jnp.asarray(score_scale, bf16)
    norm = query_lanes(part_ref)
    for b in range(0, VS, VB):
        at = slice(b, b + VB)
        p = jnp.exp(products(rows, at, q) - norm)
        if b == 0:
            p = jnp.concatenate([jnp.where(is_pair(pos_ref), 0.0, p[:PAIRS]), p[PAIRS:]], axis=0)
        weight[at, :] = p.astype(bf16)
    o_ref[...] = mm(turned[...], weight[...]).T.astype(bf16)


def vec_kernel(first, n, pos_ref, rows, parts_ref, q_ref, g_ref, lse, coef):
    @pl.when(pl.program_id(0) == 0)
    def _():
        top = parts_ref[0]
        for a in range(1, NA):
            top = jnp.maximum(top, parts_ref[a])
        total = jnp.exp(parts_ref[0] - top)
        for a in range(1, NA):
            total = total + jnp.exp(parts_ref[a] - top)
        lse[...] = top + jnp.log(total)
        g_ref[...] = jnp.zeros_like(g_ref)

    q = q_ref[...]
    scaled = q * jnp.asarray(score_scale, bf16)
    norm = query_lanes(lse)
    for b in range(0, n, 2):
        m = min(2, n - b) * PAIRS
        at = slice((first + b) * PAIRS, (first + b) * PAIRS + m)
        p = jnp.exp(products(rows, at, scaled) - norm)
        if first == 0:
            p = jnp.where(is_pair(pos_ref), p - 1.0, p)
        coef[b * PAIRS : b * PAIRS + m, :] = p.astype(bf16)
    for b in range(0, n, 2):
        m = min(2, n - b)
        g = mm(coef[b * PAIRS : (b + m) * PAIRS, :], q)
        for k in range(m):
            g_ref[b + k] += g[k * PAIRS : (k + 1) * PAIRS]


def combine_kernel(got_ref, parts_ref, q_ref, pay_ref, out_ref):
    parts = parts_ref[...]
    top = jnp.max(parts, axis=0, keepdims=True)
    lse = top + jnp.log(jnp.sum(jnp.exp(parts - top), axis=0, keepdims=True))
    shares = jnp.exp(parts - lse)
    q = q_ref[...].astype(f32)
    vec = pay_ref[0:PAIRS, :].astype(f32)
    line = pay_ref[PAIRS : PAIRS + 16, :].astype(f32)[0:1, :]
    own = jnp.sum(q * vec, axis=1, keepdims=True) * score_scale - column(line, PAIRS) - column(lse, PAIRS)
    total = (jnp.exp(own) - 1.0).astype(bf16).astype(f32) * vec
    for a in range(NA):
        total = total + got_ref[a].astype(f32) * column(shares[a : a + 1], PAIRS)
    out_ref[...] = total * score_scale


def back_kernel(*refs):
    parts, (emb_ref, hid_ref, w_out_ref, place_ref), out_ref = refs[:4], refs[4:8], refs[-1]
    total = parts[0][...]
    for part in parts[1:]:
        total = total + part[...]
    grad = (total * score_scale).astype(bf16)
    hid = hid_ref[...]
    hg = jnp.where(hid.astype(f32) > 0.0, mm(grad, w_out_ref[...], NT), 0.0).astype(bf16)
    scatter = (iota((OWNERS * SLOT, PAIRS), 0) == place_ref[:, 0:PAIRS]).astype(f32).astype(bf16)
    slots = mm(scatter, grad).reshape(16, 2, SLOT, E)
    pieces = []
    for part in (mm(hid, grad, TN), mm(emb_ref[...], hg, TN)):
        n = part.shape[0] // 8
        tiles = [part[:, k : k + 128].reshape(n, 1, 8, 128) for k in range(0, part.shape[1], 128)]
        pieces.append(jnp.concatenate(tiles, axis=1).reshape(16, 4, 2, 8, 128))
    top = iota((16, 8, 128), 1) < 4
    for c in range(2):
        left, right = slots[:, c, :, 0:128], slots[:, c, :, 128:E]
        for z in range(4):
            w0, w1 = pieces[c][:, z, 0], pieces[c][:, z, 1]
            rolled = jnp.concatenate([w1[:, 4:8], w1[:, 0:4]], axis=1)
            rows = [
                left[:, 0:8],
                jnp.where(top, left[:, 8:16], w0),
                right[:, 0:8],
                jnp.where(top, right[:, 8:16], w1),
                jnp.where(top, w0, rolled),
            ]
            out_ref[:, c, z] = jnp.concatenate(rows, axis=1).astype(bf16)


def sum_kernel(got_ref, out_ref):
    total = jnp.sum(got_ref[...].astype(f32), axis=0)
    total = jnp.concatenate([total[32:36], total[12:16], total[36:40], total[28:32]], axis=0)
    out_ref[...] = jnp.broadcast_to(total.astype(bf16)[None], (128, SLOT, 128))


TB = 512


def active_kernel(table_ref, w_in_ref, active_ref):
    hid = jnp.maximum(mm(table_ref[...].astype(bf16), w_in_ref[...]), 0.0).astype(bf16)
    active_ref[...] = (hid.astype(f32) > 0.0).astype(f32).astype(bf16)


def update_kernel(ids_ref, got_ref, table_ref, accum_ref, active_ref, w_in_ref, w_out_ref, table_out, accum_out):
    base = pl.program_id(0) * TB
    onehot = (ids_ref[...] == iota((TB, 128 * SLOT), 0) + base).astype(f32).astype(bf16)
    vals = jnp.concatenate([got_ref[:, 0:SLOT, :], got_ref[:, SLOT : 2 * SLOT, :]], axis=2).reshape(128 * SLOT, E)
    vg = mm(onehot, vals)
    high = vg.astype(bf16)
    low = (vg - high.astype(f32)).astype(bf16)
    table = table_ref[...]
    back = mm(high, w_out_ref[...], NT) + mm(low, w_out_ref[...], NT)
    hg = jnp.where(active_ref[...].astype(f32) > 0.0, back, 0.0).astype(bf16)
    g = vg + mm(hg, w_in_ref[...], NT)
    acc = accum_ref[...] + g * g
    accum_out[...] = acc
    table_out[...] = table - learn_rate * g / jnp.sqrt(acc)


def a2a(x, axes):
    return lax.all_to_all(x, axes, split_axis=0, concat_axis=0, tiled=True)


def shift(x, axis, k):
    n = 2 if axis == "c" else 4
    return lax.ppermute(x, axis, [(i, (i + k) % n) for i in range(n)])


def whole(n):
    return [pl.BlockSpec(memory_space=VMEM)] * n


def unread(n):
    return [pl.BlockSpec(memory_space=pl.ANY)] * n


def const(*shape):
    return pl.BlockSpec(shape, lambda *_: (0,) * len(shape))


def local(queries, item_owner, item_row, log_freq, table, accum, w_in, w_out):
    here_x = lax.axis_index("x").astype(i32)
    here_z = lax.axis_index("z").astype(i32)
    req, place, pick = call(
        slots_kernel,
        (
            sds((OWNERS, 128), i32),
            sds((1, 256), i32),
            sds((PAIRS, OWNERS * SLOT), bf16),
        ),
        in_specs=whole(2),
        out_specs=tuple(whole(3)),
        scratch_shapes=[pltpu.VMEM((8, 256), i32)],
    )(item_owner.reshape(1, PAIRS), item_row.reshape(1, PAIRS))
    asked = a2a(req.reshape(OWNERS, 1, 128), SHARD)
    early = call(
        pass_kernel,
        sds((PAIRS, E), bf16),
        cost=(COST, 1 << 20, 0),
        limit=SMALL,
        in_specs=whole(1) + unread(1),
        out_specs=whole(1)[0],
    )(queries, req)
    blocks = [queries] + [shift(early, "x", 4 - k) for k in range(1, 4)]
    ids = asked[:, 0, :SLOT].astype(f32).reshape(OWNERS * SLOT // 128, 128)
    ids = jnp.pad(ids, ((0, 8 - OWNERS * SLOT // 128), (0, 0)))
    wanted = jnp.maximum(asked[:, 0, :SLOT].reshape(OWNERS * SLOT), 0)
    picked = table.at[wanted].get(mode="promise_in_bounds").astype(bf16)
    slab = call(
        slab_kernel,
        sds((QB, E), bf16),
        cost=(COST, 1 << 20, 0),
        limit=SMALL,
        in_specs=[pl.BlockSpec(memory_space=pltpu.MemorySpace.SMEM)] + whole(4) + unread(1),
        out_specs=whole(1)[0],
    )(here_x.reshape(1), *blocks, picked)
    above, below = shift(slab, "z", 3), shift(slab, "z", 1)
    half = QB // 2
    far = [shift(above[:half], "z", 3), shift(below[half:], "z", 1)]
    all_q = jnp.zeros((QS, E), bf16)
    for k, block in ((0, slab), (1, above), (3, below), (2, jnp.concatenate(far, axis=0))):
        all_q = lax.dynamic_update_slice(all_q, block, ((here_z + k) % 4 * QB, 0))
    got = a2a(picked.reshape(OWNERS, SLOT, E), SHARD).reshape(OWNERS * SLOT, E)
    freq_row = jnp.pad(log_freq.reshape(1, PAIRS), ((0, 15), (0, 256 - PAIRS)))
    emb, hid, pay = call(
        tower_kernel,
        (sds((PAIRS, E), bf16), sds((PAIRS, H), bf16), sds((PAIRS + 16, E), bf16)),
        cost=(24 << 30, 1 << 20, 0),
        in_specs=whole(5),
        out_specs=tuple(whole(3)),
    )(got, pick, w_in, w_out, freq_row)
    vecs = [pay] + [shift(pay, "y", k) for k in range(1, 4)]
    vecs = vecs + [shift(v, "c", 1) for v in vecs]

    sent_lse, part_lse, vec_rows = call(
        score_kernel,
        (HBM((NA, SENT, 128), f32), sds((LINES, 128), f32), sds((VS, E + 128), bf16)),
        cost=(2 * VS * QS * E, VS * QS * 2, VS * QS),
        limit=LIMIT,
        in_specs=whole(NB + 2),
        out_specs=tuple(whole(3)),
        scratch_shapes=[pltpu.VMEM((VS, PB), f32)] * 2,
    )(*vecs, all_q, ids)
    all_lse = a2a(sent_lse, A)
    here = here_z * 4 + here_x
    o = call(
        query_kernel,
        HBM((QS, E), bf16),
        cost=(4 * VS * QS * E, VS * QS, VS * QS),
        limit=LIMIT,
        grid_spec=pltpu.PrefetchScalarGridSpec(
            num_scalar_prefetch=1,
            grid=(QS // QB,),
            in_specs=[
                const(VS, E + 128),
                const(LINES, 128),
                pl.BlockSpec((QB, E), lambda i, pos: (i, 0)),
            ],
            out_specs=pl.BlockSpec((QB, E), lambda i, pos: (i, 0)),
            scratch_shapes=[
                pltpu.VMEM((E, VS), bf16),
                pltpu.VMEM((VS, QB), bf16),
            ],
        ),
    )(here.reshape(1), vec_rows, part_lse, all_q)

    def vec_grads(first, n, wait):
        first_lse, _ = lax.optimization_barrier((all_lse, wait))
        return call(
            functools.partial(vec_kernel, first, n),
            sds((n, PAIRS, E), f32),
            cost=(4 * n * PAIRS * QS * E, n * PAIRS * QS, n * PAIRS * QS),
            limit=LIMIT,
            grid_spec=pltpu.PrefetchScalarGridSpec(
                num_scalar_prefetch=1,
                grid=(QS // QB,),
                in_specs=[
                    const(VS, E + 128),
                    const(NA, SENT, 128),
                    pl.BlockSpec((QB, E), lambda i, pos: (i, 0)),
                ],
                out_specs=const(n, PAIRS, E),
                scratch_shapes=[
                    pltpu.VMEM((SENT, 128), f32),
                    pltpu.VMEM((n * PAIRS, QB), bf16),
                ],
            ),
        )(here.reshape(1), vec_rows, first_lse, all_q)

    o_got = a2a(o.reshape(NA, PAIRS, E), A)

    other = vec_grads(4, 4, o)
    same = vec_grads(1, 3, other)
    from_core = shift(other, "c", 1)
    sums = [same[k - 1] + from_core[k] for k in range(1, 4)]
    parts = [shift(sums[k - 1], "y", 4 - k) for k in range(1, 4)]
    mine = vec_grads(0, 1, sums[2])
    parts = [mine.reshape(PAIRS, E) + from_core[0]] + parts
    parts[0], o_got = lax.optimization_barrier((parts[0], o_got))
    out = call(
        back_kernel,
        sds((16, 2, 4, PACK, 128), bf16),
        limit=LARGE,
        in_specs=whole(8),
        out_specs=whole(1)[0],
    )(*parts, emb, hid, w_out, place)
    back = a2a(out.reshape(128, PACK, 128), ALL)

    own = lax.dynamic_slice(all_lse[:, :LINES].reshape(NA, QS), (0, here * PAIRS), (NA, PAIRS))
    query_grad = call(
        combine_kernel,
        sds((PAIRS, E), f32),
        limit=SMALL,
        in_specs=whole(4),
        out_specs=whole(1)[0],
    )(o_got, jnp.pad(own, ((0, 0), (0, 256 - PAIRS))), queries, pay)

    active = call(
        active_kernel,
        sds((ROWS, H), bf16),
        cost=(2 * ROWS * E * H, ROWS * (E * 4 + H * 2), 0),
        limit=SMALL,
        grid=(ROWS // TB,),
        in_specs=[pl.BlockSpec((TB, E), lambda i: (i, 0)), const(E, H)],
        out_specs=pl.BlockSpec((TB, H), lambda i: (i, 0)),
    )(table, w_in)
    back, query_grad, active = lax.optimization_barrier((back, query_grad, active))
    w_sum = call(
        sum_kernel,
        HBM((128, SLOT, 128), bf16),
        limit=LIMIT,
        in_specs=whole(1),
        out_specs=whole(1)[0],
    )(back)
    w_all = a2a(w_sum, ALL).reshape(16, 2, 4, SLOT, 128).astype(f32)
    row_ids = all_lse.reshape(4, 4, SENT, 128)[:, :, LINES : LINES + 4]
    row_ids = lax.dynamic_index_in_dim(row_ids, here_x, axis=1, keepdims=False)
    row_ids = row_ids.reshape(4, OWNERS, SLOT).transpose(1, 0, 2).reshape(1, 128 * SLOT).astype(i32)
    table_new, accum_new = call(
        update_kernel,
        (sds((ROWS, E), f32), sds((ROWS, E), f32)),
        cost=(4 * ROWS * 2048 * E, 4 * ROWS * E * 4, 0),
        limit=LARGE,
        grid=(ROWS // TB,),
        in_specs=[
            const(1, 128 * SLOT),
            const(128, PACK, 128),
            pl.BlockSpec((TB, E), lambda i: (i, 0)),
            pl.BlockSpec((TB, E), lambda i: (i, 0)),
            pl.BlockSpec((TB, H), lambda i: (i, 0)),
            const(E, H),
            const(H, E),
        ],
        out_specs=(
            pl.BlockSpec((TB, E), lambda i: (i, 0)),
            pl.BlockSpec((TB, E), lambda i: (i, 0)),
        ),
    )(row_ids, back, table, accum, active, w_in, w_out)

    def tiles(x, rows, cols):
        return x.reshape(rows // 8, cols // 128, 8, 128).transpose(0, 2, 1, 3).reshape(rows, cols)

    w_out_grad = tiles(w_all[:, 0], H, E)
    w_in_grad = tiles(w_all[:, 1], E, H)
    return query_grad, table_new, accum_new, w_in_grad, w_out_grad


def solution(mesh):
    fine = Mesh(mesh.devices.reshape(4, 4, 2, 4), ALL)
    return jax.shard_map(
        local,
        mesh=fine,
        in_specs=(
            P(ALL, None),
            P(ALL, None),
            P(ALL),
            P(ALL),
            P(SHARD, None),
            P(SHARD, None),
            P(),
            P(),
        ),
        out_specs=(P(ALL, None), P(SHARD, None), P(SHARD, None), P(), P()),
        check_vma=False,
    )
```
